32 devices in a mesh: dp: 16 (over z, x, core), tensor: 2 (over y).
Axes of the slice: x: 2, y: 2, z: 4, core: 2. Of those that a mesh axis runs over, the one named last changes fastest.
Arguments:
- queries: bfloat16 [16384, 4096], P('dp', 'tensor'), may hold values from -6 to 6
- out_grad: bfloat16 [16384, 4096], P('dp', 'tensor'), may hold values from -6 to 6
- target_len: int32 [16], P('dp'), may hold values from 1 to 1024, 12288 in all
- encoded: bfloat16 [2048, 4096], P('dp', 'tensor'), may hold values from -6 to 6
- row_owner: int32 [2048, 1], P('dp'), may hold values from 0 to 15; in each aligned block of 128 rows (0 to 127, 128 to 255, ...) at most 16 rows name the same one
- projections: bfloat16 [2, 4096, 4096], P(None, 'dp', 'tensor'), may hold values from -0.09375 to 0.09375
- velocity: float32 [2, 4096, 4096], P(None, 'dp', 'tensor'), may hold values from -0.046875 to 0.046875
Outputs:
- query_grad: bfloat16 [16384, 4096], P('dp', 'tensor')
- encoded_grad: bfloat16 [2048, 4096], P('dp', 'tensor')
The draws below stay inside these ranges and needn't reach their ends.
Inputs may be any that keep to these rules, and one draw needn't show every extreme that they name: row_owner[r, 0] names the sample whose decoder positions attend to encoder row r; sample s has its 1024 query rows on index s of dp. Among the 128 rows of one index of dp at most 16 name the same sample, exactly 16 do for some sample, and every sample is named by some row. `target_len`: some sample has all 1024 positions live.
All inputs are finite; a program needn't handle non-finite values. No bound on the sum of `target_len` on one device may be relied on, other than what follows from the above.
Results may differ from the reference program's by a relative error of at most 0.014.
Values may be sent and summed in bfloat16 or wider, within the bound.
No kernel may reach another device: no remote copies, remote signals or barrier semaphores. Data moves between devices by JAX's collectives and lax.ppermute only.
A program may use at most 128 MiB of HBM per device.

```python
import math
import jax
import jax.numpy as jnp
import numpy as np
from jax import lax

D = 4096
HEADS = 16
HD = 256
TQ = 1024
TS = 128
CAP = 16
SLOTS = 256
HH = 4096
TOKENS = 16384
SRC = 2048
N_DP = 16
N_TENSOR = 2


def steps_of(key, extent, split, least, largest):
    factor_of, own = 1.0, jax.random.fold_in(key, 6)
    for axis_at, shards_of in split:
        draws = jnp.exp(jax.random.uniform(jax.random.fold_in(own, axis_at), (shards_of,), jnp.float32, least / len(split), largest / len(split)))
        factor_of = factor_of * jnp.repeat(draws, extent[axis_at] // shards_of).reshape([-1 if axis == axis_at else 1 for axis in range(len(extent))])
    return factor_of


def profile(number_of, total, most, skew):
    portions = [(1 << 20) // math.isqrt(rank ** skew) + 1 for rank in range(2, number_of + 1)]
    spare, given = total - most - (number_of - 1), [1] * (number_of - 1)
    while spare > 0:
        candidates = [i for i in range(number_of - 1) if given[i] < most]
        mass, left = sum([portions[i] for i in candidates]), spare
        for i in candidates:
            addition = min(most - given[i], max(1, left * portions[i] // mass), spare)
            given[i] = given[i] + addition
            spare = spare - addition
    return np.array([most] + given)


def ragged(key, number_of, total, most, lean):
    if number_of == 2:
        one = jax.random.randint(key, (), max(1, total - most), min(most, total - 1) + 1)
        return jnp.stack([one, total - one])
    tallies = jnp.asarray(profile(number_of, total, most, lean), jnp.int32)
    twos = (number_of - 1) // 2
    source_of, receiver = tallies[1:1 + 2 * twos:2], tallies[2:2 + 2 * twos:2]
    room = jnp.minimum(source_of - 1, most - receiver)
    moved = jax.random.randint(jax.random.fold_in(key, 1), (twos,), 0, 1 << 20) % (room + 1)
    tallies = tallies.at[1:1 + 2 * twos:2].set(source_of - moved).at[2:2 + 2 * twos:2].set(receiver + moved)
    return tallies[jax.random.permutation(jax.random.fold_in(key, 2), number_of)]


def assign_block(rng, own, number, rows, amount, top, limit, skew):
    sequence = jax.random.permutation(rng, amount)
    heavy_load, ordinary = load_shares(amount, rows * top, limit, skew, True), load_shares(amount, rows * top, limit, skew, False)
    places = jnp.arange(amount)

    def named(sizes, turn):
        used = int((sizes > 0).sum())
        fixed = max(1, used // 4)
        moved = fixed + (places - fixed + turn * (used - fixed)) % max(1, amount - fixed)
        return jnp.zeros((amount,), jnp.int32).at[sequence[jnp.where(places < fixed, places, moved)]].set(jnp.asarray(sizes, jnp.int32))

    sizes = jnp.where(number % 4 == 0, named(heavy_load, number // 4), named(ordinary, number - number // 4 - 1))
    mixed = jax.random.permutation(jax.random.fold_in(own, 3), amount)
    donor, receiver = mixed[0:amount // 2 * 2:2], mixed[1:amount // 2 * 2:2]
    slack = jnp.minimum(sizes[donor] - 1, limit - sizes[receiver]) // 2
    slack = jnp.where((donor == sequence[0]) | (receiver == sequence[0]) | (sizes[receiver] == 0), 0, jnp.maximum(slack, 0))
    moved = jax.random.randint(jax.random.fold_in(own, 4), (amount // 2,), 0, 1 << 20) % (slack + 1)
    sizes = sizes.at[donor].add(-moved).at[receiver].add(moved)
    items = jnp.searchsorted(jnp.cumsum(sizes), jnp.arange(rows * top), side="right").astype(jnp.int32)
    listing = items.reshape(top, rows).T
    listing = listing[jax.random.permutation(jax.random.fold_in(own, 1), rows)]
    turn = jax.random.randint(jax.random.fold_in(own, 2), (rows, 1), 0, top)
    return jnp.take_along_axis(listing, (jnp.arange(top)[None, :] + turn) % top, axis=1)


def load_shares(amount, total, reach, lean, full):
    portions = [(1 << 20) // math.isqrt(grade ** lean) + 1 for grade in range(1, amount + 1)]
    largest = reach if full else min(reach, max(-(-total // amount), total * portions[0] // sum(portions)))
    least = 1 if total - largest >= amount - 1 else 0
    given, surplus = [largest] + [least] * (amount - 1), total - largest - least * (amount - 1)
    while surplus > 0:
        free = [i for i in range(1, amount) if given[i] < largest] or [i for i in range(1, amount) if given[i] < reach]
        pool, remaining = sum([portions[i] for i in free]), surplus
        for i in free:
            more = min(reach - given[i], max(1, remaining * portions[i] // pool), surplus)
            given[i] = given[i] + more
            surplus = surplus - more
    return np.array(given)


def normal_values(key, shape, scale, reach, pieces=(), kind=jnp.bfloat16):
    loudness = steps_of(key, shape, pieces, -0.22, 0.18) if pieces else 1.0
    drawn = jax.random.normal(key, shape, jnp.float32) * scale * loudness
    return jnp.minimum(jnp.maximum(drawn, -reach), reach).astype(kind)


def setup_inputs(seed: int = 0) -> dict:
    arg_keys = jax.random.split(jax.random.key(seed), 8)
    queries = normal_values(arg_keys[0], (TOKENS, HH), 1.0, 6.0, ((0, 16), (1, 2)))
    out_grad = normal_values(arg_keys[1], (TOKENS, HH), 1.0, 6.0, ((0, 16), (1, 2)))
    target_len = ragged(arg_keys[2], N_DP, N_DP * TQ * 3 // 4, TQ, 1).astype(jnp.int32)
    encoded = normal_values(arg_keys[3], (SRC, D), 1.0, 6.0, ((0, 16), (1, 2)))
    row_owner_keys = jax.random.split(jax.random.fold_in(arg_keys[4], 1), SRC // TS)
    row_owner_turns = jax.random.permutation(jax.random.fold_in(arg_keys[4], 3), SRC // TS)
    row_owner = jax.vmap(lambda own, number: assign_block(jax.random.fold_in(arg_keys[4], 2), own, number, TS, N_DP, 1, CAP, 2))(row_owner_keys, row_owner_turns).reshape((SRC, 1))
    projections = normal_values(arg_keys[5], (2, D, HH), D ** -0.5, 0.09375, ((1, 16), (2, 2)))
    velocity = normal_values(arg_keys[6], (2, D, HH), (4 * D) ** -0.5, 0.046875, ((1, 16), (2, 2)), jnp.float32)
    return dict(queries=queries, out_grad=out_grad, target_len=target_len, encoded=encoded, row_owner=row_owner, projections=projections, velocity=velocity)


cap_limit = 10.0

def rounded(value):
    return lax.optimization_barrier(value.astype(jnp.bfloat16)).astype(jnp.float32)

def reference(queries, out_grad, target_len, encoded, row_owner, projections, velocity):
    predicted = (projections.astype(jnp.float32) - velocity).astype(jnp.bfloat16)
    keys = jnp.dot(encoded, predicted[0], preferred_element_type=jnp.float32).astype(jnp.bfloat16)
    values = jnp.dot(encoded, predicted[1], preferred_element_type=jnp.float32).astype(jnp.bfloat16)
    position = jnp.arange(TOKENS, dtype=jnp.int32)
    sample = position // TQ
    alive_rows = position % TQ < target_len[sample]
    live_grad = jnp.where(alive_rows[:, None], out_grad, jnp.zeros_like(out_grad))
    labels = row_owner[:, 0].astype(jnp.int32)
    sorted_rows = jnp.argsort(labels, stable=True).astype(jnp.int32)
    counts = lax.optimization_barrier(jnp.sum((labels[None, :] == jnp.arange(N_DP, dtype=jnp.int32)[:, None]).astype(jnp.int32), axis=1))
    starts = (jnp.cumsum(counts) - counts).astype(jnp.int32)
    slot_ids = jnp.arange(SLOTS, dtype=jnp.int32)
    score_scale = 1.0 / math.sqrt(HD)

    def one_sample(sample_id):
        usable = (slot_ids < counts[sample_id]).astype(jnp.float32)
        picked = sorted_rows[jnp.clip(starts[sample_id] + slot_ids, 0, SRC - 1)]
        key_heads = keys[picked].astype(jnp.float32).reshape(SLOTS, HEADS, HD)
        value_heads = values[picked].astype(jnp.float32).reshape(SLOTS, HEADS, HD)
        first_row = (sample_id * TQ).astype(jnp.int32)
        query_heads = lax.dynamic_slice_in_dim(queries, first_row, TQ, 0).astype(jnp.float32).reshape(TQ, HEADS, HD)
        grad_heads = lax.dynamic_slice_in_dim(live_grad, first_row, TQ, 0).astype(jnp.float32).reshape(TQ, HEADS, HD)
        raw_scores = jnp.einsum('qhd,khd->hqk', query_heads, key_heads) * score_scale
        capped = cap_limit * jnp.tanh(raw_scores / cap_limit)
        exp_terms = jnp.exp(capped) * usable[None, None, :]
        attention = exp_terms / lax.optimization_barrier(jnp.sum(exp_terms, axis=-1, keepdims=True))
        prob_grad = jnp.einsum('qhd,khd->hqk', grad_heads, value_heads)
        row_term = lax.optimization_barrier(jnp.sum(attention * prob_grad, axis=-1, keepdims=True))
        score_grad = rounded(attention * (prob_grad - row_term) * (1.0 - (capped / cap_limit) ** 2) * score_scale)
        rounded_attention = rounded(attention)
        query_block = jnp.einsum('hqk,khd->qhd', score_grad, key_heads).reshape(TQ, HH).astype(jnp.bfloat16)
        key_block = jnp.einsum('hqk,qhd->khd', score_grad, query_heads).reshape(SLOTS, HH).astype(jnp.bfloat16)
        value_block = jnp.einsum('hqk,qhd->khd', rounded_attention, grad_heads).reshape(SLOTS, HH).astype(jnp.bfloat16)
        return (query_block, key_block, value_block, picked)
    query_all, key_all, value_all, picked_all = lax.map(one_sample, jnp.arange(N_DP, dtype=jnp.int32))
    query_grad = query_all.reshape(TOKENS, HH)
    flat_rows = picked_all.reshape(-1)
    key_grad = jnp.zeros((SRC, HH), jnp.float32).at[flat_rows].add(key_all.reshape(-1, HH).astype(jnp.float32)).astype(jnp.bfloat16)
    value_grad = jnp.zeros((SRC, HH), jnp.float32).at[flat_rows].add(value_all.reshape(-1, HH).astype(jnp.float32)).astype(jnp.bfloat16)
    group_cols = HH // N_TENSOR
    summed = jnp.zeros((SRC, D), jnp.float32)
    for group_id in range(N_TENSOR):
        low = group_id * group_cols
        high = low + group_cols
        partial_value = jnp.dot(key_grad[:, low:high], predicted[0][:, low:high].T, preferred_element_type=jnp.float32)
        partial_value = partial_value + jnp.dot(value_grad[:, low:high], predicted[1][:, low:high].T, preferred_element_type=jnp.float32)
        summed = summed + rounded(partial_value)
    return (query_grad, summed.astype(jnp.bfloat16))
```

```python
import functools
import math

import jax
import jax.numpy as jnp
from jax import lax
from jax.experimental import pallas as pl
from jax.experimental.pallas import tpu as pltpu
from jax.sharding import PartitionSpec as P

HD = 256
CAP_LIMIT = 10.0
VMEM_LIMIT = 48 * 1024 * 1024


def slot_table(labels, capacity, peer_count):
    targets = (labels[:, None] == jnp.arange(peer_count, dtype=jnp.int32)[None, :]).astype(
        jnp.int32
    )
    before = jnp.cumsum(targets, axis=0) - targets
    rank_in = jnp.sum(before * targets, axis=1)
    slot_index = labels * capacity + rank_in
    placement = jnp.arange(peer_count * capacity, dtype=jnp.int32)[:, None] == slot_index[None, :]
    return placement.astype(jnp.bfloat16)


def split_heads(head_count):
    if head_count < 4:
        return [1] * head_count
    sizes = [2] * (head_count // 2)
    if head_count % 2:
        sizes.append(1)
    return sizes


def line_index(step, pos, line):
    return lax.rem(pos[0] - step + line, line)


def project_kernel(pos, rows, own, sibling, mine, other, total):
    step = pl.program_id(0)
    x, core = pos[1], pos[2]

    @pl.when(step == 0)
    def _():
        mine[...] = jnp.zeros_like(mine)
        total[...] = jnp.zeros_like(total)

    for x_at, result in ((1 - x, total), (x, mine)):
        from_own, from_sibling = rows[0, core, x_at], rows[0, 1 - core, x_at]
        for side in range(2):
            result[side] += jnp.dot(
                from_own, own[0, side], preferred_element_type=jnp.float32
            ) + jnp.dot(from_sibling, sibling[0, side], preferred_element_type=jnp.float32)

    @pl.when(step == pl.num_programs(0) - 1)
    def _():
        other[...] = total[...].astype(other.dtype)


def project(pos, rows, own, sibling, tensor_count):
    line, _, depth, width = own.shape
    slots = rows.shape[3]
    per_tensor = line // tensor_count

    def rows_at(step, pos):
        z = line_index(step, pos, line)
        shift = lax.rem(pos[3] - z // per_tensor + tensor_count, tensor_count)
        return (shift * per_tensor + lax.rem(z, per_tensor), 0, 0, 0, 0)

    weight_spec = pl.BlockSpec((1, 2, depth, width), lambda step, pos: (step, 0, 0, 0))
    whole = pl.BlockSpec((2, slots, width), lambda step, pos: (0, 0, 0))
    return pl.pallas_call(
        project_kernel,
        grid_spec=pltpu.PrefetchScalarGridSpec(
            num_scalar_prefetch=1,
            grid=(line,),
            in_specs=[
                pl.BlockSpec((1, 2, 2, slots, depth), rows_at),
                weight_spec,
                weight_spec,
            ],
            out_specs=[whole, whole],
            scratch_shapes=[pltpu.VMEM((2, slots, width), jnp.float32)],
        ),
        out_shape=(
            jax.ShapeDtypeStruct((2, slots, width), jnp.float32),
            jax.ShapeDtypeStruct((2, slots, width), jnp.bfloat16),
        ),
        compiler_params=pltpu.CompilerParams(vmem_limit_bytes=VMEM_LIMIT),
        cost_estimate=pl.CostEstimate(
            flops=2 * 2 * slots * 2 * line * depth * 2 * width,
            bytes_accessed=2 * own.size * 2 + rows.size * 2 + 6 * 2 * slots * width,
            transcendentals=0,
        ),
        name="project",
    )(pos, rows, own, sibling)


def attend_kernel(block, live, usable, queries, grads, mine, received, *rest):
    query_grad, pair_grad, key_total, value_total = rest[-4:]
    keys = (mine[0] + received[0].astype(jnp.float32)).astype(jnp.bfloat16)
    values = (mine[1] + received[1].astype(jnp.float32)).astype(jnp.bfloat16)
    scale = 1.0 / math.sqrt(HD)
    mask = usable[...]
    last_dims = (((1,), (1,)), ((), ()))
    query_count = queries.shape[0]
    for first in range(0, query_count, block):
        at = pl.ds(first, block)
        q = queries[at, :]
        position = first + lax.broadcasted_iota(jnp.int32, (block, 1), 0)
        g = grads[at, :]
        g = jnp.where(position < live[0], g, jnp.zeros_like(g))
        raw = lax.dot_general(keys, q, last_dims, preferred_element_type=jnp.float32)
        bent = jnp.tanh(raw * (scale / CAP_LIMIT))
        terms = jnp.exp(bent * CAP_LIMIT) * mask
        attention = terms * (1.0 / jnp.sum(terms, axis=0, keepdims=True))
        prob_grad = lax.dot_general(values, g, last_dims, preferred_element_type=jnp.float32)
        row_term = jnp.sum(attention * prob_grad, axis=0, keepdims=True)
        score_grad = (
            attention * (prob_grad - row_term) * ((1.0 - bent * bent) * scale)
        ).astype(jnp.bfloat16)
        rounded = attention.astype(jnp.bfloat16)
        query_grad[at, :] = lax.dot_general(
            score_grad, keys, (((0,), (0,)), ((), ())), preferred_element_type=jnp.float32
        ).astype(jnp.bfloat16)
        key_block = jnp.dot(score_grad, q, preferred_element_type=jnp.float32)
        value_block = jnp.dot(rounded, g, preferred_element_type=jnp.float32)
        if first == 0:
            key_total[...] = key_block
            value_total[...] = value_block
        else:
            key_total[...] += key_block
            value_total[...] += value_block
    pair_grad[0] = key_total[...].astype(jnp.bfloat16)
    pair_grad[1] = value_total[...].astype(jnp.bfloat16)


def attend(live, usable, queries, grads, mine, received, first_head, earlier):
    query_count, width = queries.shape
    _, slots, chunk = mine.shape
    heads = chunk // HD
    block = min(256, query_count)
    columns = pl.BlockSpec((query_count, HD), lambda head: (0, first_head + head))
    pair = pl.BlockSpec((2, slots, HD), lambda head: (0, 0, head))
    operands = [live, usable, queries, grads, mine, received]
    in_specs = [
        pl.BlockSpec(memory_space=pltpu.SMEM),
        pl.BlockSpec((slots, 1), lambda head: (0, 0)),
        columns,
        columns,
        pair,
        pair,
    ]
    aliases = {}
    if earlier is not None:
        aliases = {len(operands): 0}
        operands.append(earlier)
        in_specs.append(pl.BlockSpec(memory_space=pl.ANY))
    return pl.pallas_call(
        functools.partial(attend_kernel, block),
        grid=(heads,),
        in_specs=in_specs,
        out_specs=[columns, pair],
        out_shape=(
            jax.ShapeDtypeStruct((query_count, width), jnp.bfloat16),
            jax.ShapeDtypeStruct((2, slots, chunk), jnp.bfloat16),
        ),
        scratch_shapes=[pltpu.VMEM((slots, HD), jnp.float32)] * 2,
        input_output_aliases=aliases,
        compiler_params=pltpu.CompilerParams(vmem_limit_bytes=VMEM_LIMIT),
        cost_estimate=pl.CostEstimate(
            flops=10 * query_count * slots * chunk,
            bytes_accessed=6 * query_count * chunk + 10 * 2 * slots * chunk,
            transcendentals=2 * query_count * slots * heads,
        ),
        name="attend",
    )(*operands)


def spread_kernel(pos, mine, received, own, sibling, *rest):
    result = rest[-1]
    x, core = pos[1], pos[2]
    last_dims = (((1,), (1,)), ((), ()))
    for core_at, weights in ((core, own), (1 - core, sibling)):
        for x_at, grads in ((x, mine), (1 - x, received)):
            total = lax.dot_general(
                grads[0], weights[0, 0], last_dims, preferred_element_type=jnp.float32
            ) + lax.dot_general(
                grads[1], weights[0, 1], last_dims, preferred_element_type=jnp.float32
            )
            if len(rest) > 1:
                total = total + rest[0][0, core_at, x_at]
            result[0, core_at, x_at] = total.astype(result.dtype)


def spread(pos, mine, received, own, sibling, earlier, tensor_count, final):
    line, _, depth, width = own.shape
    slots = mine.shape[1]
    per_tensor = line // tensor_count

    def result_at(step, pos):
        z = line_index(step, pos, line)
        shift = lax.rem(z // per_tensor - pos[3] + tensor_count, tensor_count)
        return (shift * per_tensor + lax.rem(z, per_tensor), 0, 0, 0, 0)

    weight_spec = pl.BlockSpec((1, 2, depth, width), lambda step, pos: (step, 0, 0, 0))
    grad_spec = pl.BlockSpec((2, slots, width), lambda step, pos: (0, 0, 0))
    result_spec = pl.BlockSpec((1, 2, 2, slots, depth), result_at)
    operands = [pos, mine, received, own, sibling]
    in_specs = [grad_spec, grad_spec, weight_spec, weight_spec]
    aliases = {}
    if earlier is not None:
        if not final:
            aliases = {len(operands): 0}
        operands.append(earlier)
        in_specs.append(result_spec)
    shape = (line, 2, 2, slots, depth)
    return pl.pallas_call(
        spread_kernel,
        grid_spec=pltpu.PrefetchScalarGridSpec(
            num_scalar_prefetch=1, grid=(line,), in_specs=in_specs, out_specs=result_spec
        ),
        out_shape=jax.ShapeDtypeStruct(shape, jnp.bfloat16 if final else jnp.float32),
        input_output_aliases=aliases,
        compiler_params=pltpu.CompilerParams(vmem_limit_bytes=VMEM_LIMIT),
        cost_estimate=pl.CostEstimate(
            flops=2 * 2 * slots * 2 * line * depth * 2 * width,
            bytes_accessed=2 * own.size * 2 + 8 * math.prod(shape) + 8 * slots * width,
            transcendentals=0,
        ),
        name="spread",
    )(*operands)


def gather_line(block, z, line, up, down):
    rising, falling = [block], [block]
    for _ in range(line - 1):
        rising.append(lax.ppermute(rising[-1], "dp", up))
        falling.append(lax.ppermute(falling[-1], "dp", down))
    parts = [block]
    for step in range(1, line):
        parts.append(jnp.where(z >= step, rising[step], falling[line - step]))
    return jnp.stack(parts)


def on_device(queries, out_grad, target_len, encoded, row_owner, projections, velocity):
    peers = lax.axis_size("dp")
    tensor_count = lax.axis_size("tensor")
    line = peers // 4
    per_tensor = line // tensor_count
    stored_rows = encoded.shape[0]
    depth = projections.shape[1]
    capacity = max(2, 2 * stored_rows // peers)
    slots = peers * capacity
    place = lax.axis_index("dp")
    tensor_at = lax.axis_index("tensor")
    z, x, core = place // 4, (place // 2) % 2, place % 2
    pos = jnp.stack([z, x, core, tensor_at]).astype(jnp.int32)
    up = [(i, i + 4) for i in range(peers - 4)]
    down = [(i + 4, i) for i in range(peers - 4)]
    x_swap = [(i, i ^ 2) for i in range(peers)]
    core_swap = [(i, i ^ 1) for i in range(peers)]

    def tensor_shift(value, shift):
        pairs = [(i, (i + shift) % tensor_count) for i in range(tensor_count)]
        return lax.ppermute(value, "tensor", pairs)

    sizes = split_heads(queries.shape[1] // HD)
    firsts = [sum(sizes[:i]) for i in range(len(sizes))]

    own_parts, sibling_parts = [], []
    for first, size in zip(firsts, sizes):
        at = slice(first * HD, (first + size) * HD)
        predicted = (projections[:, :, at].astype(jnp.float32) - velocity[:, :, at]).astype(
            jnp.bfloat16
        )
        gathered = gather_line(predicted, z, line, up, down)
        own_parts.append(gathered)
        sibling_parts.append(lax.ppermute(gathered, "dp", core_swap))

    placement = slot_table(row_owner[:, 0], capacity, peers)
    filled = jnp.sum(placement.astype(jnp.float32), axis=1).astype(jnp.bfloat16)
    outgoing = jnp.dot(placement, encoded, preferred_element_type=jnp.float32).astype(jnp.bfloat16)
    outgoing = outgoing.reshape(line, 2, 2, capacity, per_tensor, 2, 2, depth)
    outgoing = outgoing.transpose(0, 5, 2, 4, 6, 1, 3, 7).reshape(peers, -1, depth)
    incoming = lax.all_to_all(outgoing, "dp", split_axis=0, concat_axis=0, tiled=True)
    incoming_flag = lax.all_to_all(filled, "dp", split_axis=0, concat_axis=0, tiled=True)
    usable = (incoming_flag.astype(jnp.float32) > 0.5).astype(jnp.float32)[:, None]
    incoming = incoming.reshape(peers, per_tensor, 2, 2, capacity, depth)
    incoming = incoming.transpose(1, 2, 3, 0, 4, 5).reshape(per_tensor, 2, 2, slots, depth)
    rows = jnp.concatenate(
        [incoming] + [tensor_shift(incoming, shift) for shift in range(1, tensor_count)]
    )

    query_grad = None
    spread_total = None
    for index, (first, size) in enumerate(zip(firsts, sizes)):
        own, sibling = own_parts[index], sibling_parts[index]
        mine, other = project(pos, rows, own, sibling, tensor_count)
        received = lax.ppermute(other, "dp", x_swap)
        query_grad, pair_grad = attend(
            target_len, usable, queries, out_grad, mine, received, first, query_grad
        )
        pair_received = lax.ppermute(pair_grad, "dp", x_swap)
        spread_total = spread(
            pos,
            pair_grad,
            pair_received,
            own,
            sibling,
            spread_total,
            tensor_count,
            index == len(sizes) - 1,
        )

    summed = spread_total[:per_tensor].astype(jnp.float32)
    for shift in range(1, tensor_count):
        part = spread_total[shift * per_tensor : (shift + 1) * per_tensor]
        summed = summed + tensor_shift(part, shift).astype(jnp.float32)
    summed = summed.astype(jnp.bfloat16).reshape(per_tensor, 2, 2, peers, capacity, depth)
    summed = summed.transpose(3, 0, 1, 2, 4, 5).reshape(peers, -1, depth)
    returned = lax.all_to_all(summed, "dp", split_axis=0, concat_axis=0, tiled=True)
    returned = returned.reshape(line, 2, 2, per_tensor, 2, 2, capacity, depth)
    returned = returned.transpose(0, 5, 2, 6, 3, 1, 4, 7).reshape(slots, -1)
    encoded_grad = lax.dot_general(
        placement, returned, (((0,), (0,)), ((), ())), preferred_element_type=jnp.float32
    ).astype(jnp.bfloat16)
    return (query_grad, encoded_grad)


def solution(mesh):
    in_specs = (
        P("dp", "tensor"),
        P("dp", "tensor"),
        P("dp"),
        P("dp", "tensor"),
        P("dp", None),
        P(None, "dp", "tensor"),
        P(None, "dp", "tensor"),
    )
    out_specs = (P("dp", "tensor"), P("dp", "tensor"))
    return jax.shard_map(
        on_device, mesh=mesh, in_specs=in_specs, out_specs=out_specs, check_vma=False
    )
```

```python
import functools
import math

import jax
import jax.numpy as jnp
from jax import lax
from jax.experimental import pallas as pl
from jax.experimental.pallas import tpu as pltpu
from jax.sharding import PartitionSpec as P

HD = 256
CAP_LIMIT = 10.0
VMEM_LIMIT = 48 * 1024 * 1024


def slot_table(labels, capacity, peer_count):
    targets = (labels[:, None] == jnp.arange(peer_count, dtype=jnp.int32)[None, :]).astype(
        jnp.int32
    )
    before = jnp.cumsum(targets, axis=0) - targets
    rank_in = jnp.sum(before * targets, axis=1)
    slot_index = labels * capacity + rank_in
    placement = jnp.arange(peer_count * capacity, dtype=jnp.int32)[:, None] == slot_index[None, :]
    return placement.astype(jnp.bfloat16)


def split_heads(head_count):
    if head_count < 4:
        return [1] * head_count
    part = (3 * head_count) // 8
    return [head_count - part, part]


def split_units(size):
    return [2] * (size // 2) + [1] * (size % 2)


ANYWHERE = pl.BlockSpec(memory_space=pl.ANY)


def predict_kernel(weights, velocity, *rest):
    result = rest[-1]
    for side in range(2):
        result[:, side * HD : (side + 1) * HD] = (
            weights[side].astype(jnp.float32) - velocity[side]
        ).astype(jnp.bfloat16)


def predict(projections, velocity, first, size, *tokens):
    depth = projections.shape[1]
    spec = pl.BlockSpec((2, depth, HD), lambda head: (0, 0, first + head))
    return pl.pallas_call(
        predict_kernel,
        grid=(size,),
        in_specs=[spec, spec] + [ANYWHERE] * len(tokens),
        out_specs=pl.BlockSpec((depth, 2 * HD), lambda head: (0, head)),
        out_shape=jax.ShapeDtypeStruct((depth, 2 * HD * size), jnp.bfloat16),
        cost_estimate=pl.CostEstimate(
            flops=2 * depth * HD * size, bytes_accessed=16 * depth * HD * size, transcendentals=0
        ),
        name="predict",
    )(projections, velocity, *tokens)


def arrange_kernel(pos, rows, result, *, line, tensor_count):
    per_tensor = line // tensor_count
    slots, depth = rows.shape[3:]
    for x_at in range(2):
        for z in range(line):
            shift = lax.rem(pos[3] - z // per_tensor + tensor_count, tensor_count)
            for core in range(2):
                first = (2 * z + core) * depth
                result[x_at * slots : (x_at + 1) * slots, first : first + depth] = rows[
                    shift * per_tensor + z % per_tensor, core, lax.rem(pos[1] + x_at, 2)
                ]


def arrange(pos, rows, line, tensor_count):
    slots, depth = rows.shape[3:]
    return pl.pallas_call(
        functools.partial(arrange_kernel, line=line, tensor_count=tensor_count),
        in_specs=[
            pl.BlockSpec(memory_space=pltpu.SMEM),
            pl.BlockSpec(memory_space=pltpu.VMEM),
        ],
        out_specs=pl.BlockSpec(memory_space=pltpu.VMEM),
        out_shape=jax.ShapeDtypeStruct((2 * slots, 2 * line * depth), jnp.bfloat16),
        compiler_params=pltpu.CompilerParams(vmem_limit_bytes=VMEM_LIMIT),
        cost_estimate=pl.CostEstimate(
            flops=0, bytes_accessed=4 * rows.size, transcendentals=0
        ),
        name="arrange",
    )(pos, rows)


def project_kernel(rows, weights, *rest):
    mine, other = rest[-2:]
    slots = mine.shape[0]
    total = jnp.dot(rows[...], weights[...], preferred_element_type=jnp.float32)
    mine[...] = total[:slots]
    other[...] = total[slots:].astype(other.dtype)


def project(rows, weights, first, width, *tokens):
    features = weights.shape[0]
    first_block = first // HD
    slots = rows.shape[0] // 2
    result_spec = pl.BlockSpec((slots, HD), lambda at: (0, at))
    return pl.pallas_call(
        project_kernel,
        grid=(width // HD,),
        in_specs=[
            pl.BlockSpec(rows.shape, lambda at: (0, 0)),
            pl.BlockSpec((features, HD), lambda at: (0, first_block + at)),
        ]
        + [ANYWHERE] * len(tokens),
        out_specs=[result_spec, result_spec],
        out_shape=(
            jax.ShapeDtypeStruct((slots, width), jnp.float32),
            jax.ShapeDtypeStruct((slots, width), jnp.bfloat16),
        ),
        compiler_params=pltpu.CompilerParams(vmem_limit_bytes=VMEM_LIMIT),
        cost_estimate=pl.CostEstimate(
            flops=2 * 2 * slots * features * width,
            bytes_accessed=2 * features * width + rows.size * 2 + 6 * slots * width,
            transcendentals=0,
        ),
        name="project",
    )(rows, weights, *tokens)


def attend_kernel(block, live, usable, queries, grads, mine, received, *rest):
    query_grad, pair_grad, key_total, value_total = rest[-4:]
    both = (mine[...] + received[...].astype(jnp.float32)).astype(jnp.bfloat16)
    keys, values = both[:, :HD], both[:, HD:]
    scale = 1.0 / math.sqrt(HD)
    mask = usable[...]
    last_dims = (((1,), (1,)), ((), ()))
    query_count = queries.shape[0]
    for first in range(0, query_count, block):
        at = pl.ds(first, block)
        q = queries[at, :]
        position = first + lax.broadcasted_iota(jnp.int32, (block, 1), 0)
        g = grads[at, :]
        g = jnp.where(position < live[0], g, jnp.zeros_like(g))
        raw = lax.dot_general(keys, q, last_dims, preferred_element_type=jnp.float32)
        bent = jnp.tanh(raw * (scale / CAP_LIMIT))
        terms = jnp.exp(bent * CAP_LIMIT) * mask
        attention = terms * (1.0 / jnp.sum(terms, axis=0, keepdims=True))
        prob_grad = lax.dot_general(values, g, last_dims, preferred_element_type=jnp.float32)
        row_term = jnp.sum(attention * prob_grad, axis=0, keepdims=True)
        score_grad = (
            attention * (prob_grad - row_term) * ((1.0 - bent * bent) * scale)
        ).astype(jnp.bfloat16)
        rounded = attention.astype(jnp.bfloat16)
        query_grad[at, :] = lax.dot_general(
            score_grad, keys, (((0,), (0,)), ((), ())), preferred_element_type=jnp.float32
        ).astype(jnp.bfloat16)
        key_block = jnp.dot(score_grad, q, preferred_element_type=jnp.float32)
        value_block = jnp.dot(rounded, g, preferred_element_type=jnp.float32)
        if first == 0:
            key_total[...] = key_block
            value_total[...] = value_block
        else:
            key_total[...] += key_block
            value_total[...] += value_block
    pair_grad[:, :HD] = key_total[...].astype(jnp.bfloat16)
    pair_grad[:, HD:] = value_total[...].astype(jnp.bfloat16)


def attend(live, usable, queries, grads, mine, received, first_head, earlier, *tokens):
    query_count, width = queries.shape
    slots, chunk = mine.shape
    heads = chunk // (2 * HD)
    block = min(256, query_count)
    columns = pl.BlockSpec((query_count, HD), lambda head: (0, first_head + head))
    pair = pl.BlockSpec((slots, 2 * HD), lambda head: (0, head))
    operands = [live, usable, queries, grads, mine, received]
    in_specs = [
        pl.BlockSpec(memory_space=pltpu.SMEM),
        pl.BlockSpec((slots, 1), lambda head: (0, 0)),
        columns,
        columns,
        pair,
        pair,
    ]
    aliases = {}
    if earlier is not None:
        aliases = {len(operands): 0}
        operands.append(earlier)
        in_specs.append(ANYWHERE)
    operands += tokens
    in_specs += [ANYWHERE] * len(tokens)
    return pl.pallas_call(
        functools.partial(attend_kernel, block),
        grid=(heads,),
        in_specs=in_specs,
        out_specs=[columns, pair],
        out_shape=(
            jax.ShapeDtypeStruct((query_count, width), jnp.bfloat16),
            jax.ShapeDtypeStruct((slots, chunk), jnp.bfloat16),
        ),
        scratch_shapes=[pltpu.VMEM((slots, HD), jnp.float32)] * 2,
        input_output_aliases=aliases,
        compiler_params=pltpu.CompilerParams(vmem_limit_bytes=VMEM_LIMIT),
        cost_estimate=pl.CostEstimate(
            flops=5 * query_count * slots * chunk,
            bytes_accessed=3 * query_count * chunk + 10 * slots * chunk,
            transcendentals=2 * query_count * slots * heads,
        ),
        name="attend",
    )(*operands)


def spread_kernel(pos, *refs, parts, sides, earlier):
    scratch = parts if len(sides) > 1 else 0
    result, joined = refs[len(refs) - 1 - scratch], refs[len(refs) - scratch :]
    stride = len(sides) + 1
    depth = result.shape[-1]
    slots = refs[0].shape[0]

    if scratch:

        @pl.when(pl.program_id(0) == 0)
        def _():
            for part in range(parts):
                for at in range(len(sides)):
                    joined[part][at * slots : (at + 1) * slots] = refs[stride * part + at][...]

    total = None
    for part in range(parts):
        grads = joined[part] if scratch else refs[stride * part]
        term = lax.dot_general(
            grads[...],
            refs[stride * part + stride - 1][...],
            (((1,), (1,)), ((), ())),
            preferred_element_type=jnp.float32,
        )
        total = term if total is None else total + term
    for core in range(2):
        for at in range(len(sides)):
            share = total[at * slots : (at + 1) * slots, core * depth : (core + 1) * depth]
            if earlier:
                share = share + refs[stride * parts][0, core, at]
            result[0, core, at] = share.astype(result.dtype)


def spread(pos, depth, units, earlier, sides, first, count, tensor_count, dtype, *tokens):
    line = units[0][2].shape[0] // (2 * depth)
    slots = units[0][0].shape[0]
    per_tensor = line // tensor_count

    def weight_at(column):
        def index(step, pos):
            block = first + step
            return (
                lax.rem(pos[3] + block // per_tensor, tensor_count) * per_tensor
                + lax.rem(block, per_tensor),
                column,
            )

        return index

    operands, in_specs, scratch, widths = [pos], [], [], 0
    for unit in units:
        width = unit[0].shape[1]
        for side in sides:
            operands.append(unit[side])
            in_specs.append(pl.BlockSpec((slots, width), lambda step, pos: (0, 0)))
        operands.append(unit[2])
        in_specs.append(pl.BlockSpec((2 * depth, width), weight_at(unit[3] // width)))
        if len(sides) > 1:
            scratch.append(pltpu.VMEM((len(sides) * slots, width), jnp.bfloat16))
        widths += width
    block = (1, 2, len(sides), slots, depth)
    if earlier is not None:
        operands.append(earlier)
        side = sides[0] if len(sides) == 1 else 0
        in_specs.append(pl.BlockSpec(block, lambda step, pos: (first + step, 0, side, 0, 0)))
    operands += tokens
    in_specs += [ANYWHERE] * len(tokens)
    return pl.pallas_call(
        functools.partial(
            spread_kernel, parts=len(units), sides=sides, earlier=earlier is not None
        ),
        grid_spec=pltpu.PrefetchScalarGridSpec(
            num_scalar_prefetch=1,
            grid=(count,),
            in_specs=in_specs,
            out_specs=pl.BlockSpec(block, lambda step, pos: (step, 0, 0, 0, 0)),
            scratch_shapes=scratch,
        ),
        out_shape=jax.ShapeDtypeStruct((count,) + block[1:], dtype),
        compiler_params=pltpu.CompilerParams(vmem_limit_bytes=VMEM_LIMIT),
        cost_estimate=pl.CostEstimate(
            flops=2 * len(sides) * slots * 2 * count * depth * widths,
            bytes_accessed=4 * count * depth * widths + 8 * count * math.prod(block),
            transcendentals=0,
        ),
        name="spread",
    )(*operands)


def on_device(queries, out_grad, target_len, encoded, row_owner, projections, velocity):
    peers = lax.axis_size("dp")
    tensor_count = lax.axis_size("tensor")
    line = peers // 4
    per_tensor = line // tensor_count
    stored_rows = encoded.shape[0]
    depth = projections.shape[1]
    capacity = max(2, 2 * stored_rows // peers)
    slots = peers * capacity
    place = lax.axis_index("dp")
    tensor_at = lax.axis_index("tensor")
    pos = jnp.stack([place // 4, (place // 2) % 2, place % 2, tensor_at]).astype(jnp.int32)
    columns = [[i for i in range(peers) if (i // 2) % 2 == side] for side in range(2)]
    x_swap = [(i, i ^ 2) for i in range(peers)]

    def tensor_shift(value, shift):
        pairs = [(i, (i + shift) % tensor_count) for i in range(tensor_count)]
        return lax.ppermute(value, "tensor", pairs)

    placement = slot_table(row_owner[:, 0], capacity, peers)
    filled = jnp.sum(placement.astype(jnp.float32), axis=1).astype(jnp.bfloat16)
    flags = filled.reshape(line, 1, 2, 2, capacity).transpose(0, 1, 3, 4, 2)
    flags = jnp.broadcast_to(flags, (line, 2, 2, capacity, 2)).reshape(peers, capacity, 2)
    flags = jnp.pad(flags, ((0, 0), (0, 0), (0, depth - 2)))
    outgoing = jnp.dot(placement, encoded, preferred_element_type=jnp.float32).astype(jnp.bfloat16)
    outgoing = outgoing.reshape(line, 2, 2, capacity, per_tensor, 2, 2, depth)
    outgoing = outgoing.transpose(0, 5, 2, 4, 6, 1, 3, 7).reshape(peers, -1, depth)
    outgoing = jnp.concatenate([outgoing, flags], axis=1)

    parts = []
    first, token = 0, ()
    for size in split_heads(queries.shape[1] // HD):
        block = predict(projections, velocity, first, size, *token)
        gathered = lax.all_gather(block, "dp", axis=0, tiled=True, axis_index_groups=columns)
        parts.append((first, size, gathered))
        first, token = first + size, (block, outgoing)

    incoming = lax.all_to_all(outgoing, "dp", split_axis=0, concat_axis=0, tiled=True)
    usable = jnp.where(
        pos[1] == 0, incoming[:, -capacity:, 0], incoming[:, -capacity:, 1]
    ).reshape(slots, 1)
    usable = (usable.astype(jnp.float32) > 0.5).astype(jnp.float32)
    incoming = incoming[:, :-capacity].reshape(peers, per_tensor, 2, 2, capacity, depth)
    incoming = incoming.transpose(1, 2, 3, 0, 4, 5).reshape(per_tensor, 2, 2, slots, depth)
    rows = jnp.concatenate(
        [incoming] + [tensor_shift(incoming, shift) for shift in range(1, tensor_count)]
    )
    rows = arrange(pos, rows, line, tensor_count)

    query_grad, token, units, early = None, (), [], None
    for at, (first, size, weights) in enumerate(parts):
        final = at == len(parts) - 1
        if final:
            early = spread(
                pos, depth, units, None, (0, 1), 0, line, tensor_count, jnp.float32
            )
            units = []
        products, column = [], 0
        for heads in split_units(size):
            width = 2 * HD * heads
            mine, other = project(rows, weights, column, width, *token)
            products.append((column, mine, lax.ppermute(other, "dp", x_swap)))
            column += width
        for column, mine, received in products:
            query_grad, pair_grad = attend(
                target_len,
                usable,
                queries,
                out_grad,
                mine,
                received,
                first + column // (2 * HD),
                query_grad,
                *((early,) if final else ()),
            )
            units.append((pair_grad, lax.ppermute(pair_grad, "dp", x_swap), weights, column))
            token = (pair_grad,)

    def finish(side, *tokens):
        sent = spread(
            pos, depth, units, early, (side,), per_tensor, line - per_tensor, tensor_count,
            jnp.bfloat16, *tokens,
        )
        passed = [
            tensor_shift(sent[(shift - 1) * per_tensor : shift * per_tensor], shift)
            for shift in range(1, tensor_count)
        ]
        kept = spread(
            pos, depth, units, early, (side,), 0, per_tensor, tensor_count, jnp.float32, sent
        )
        return kept, passed

    def send_home(kept, passed):
        for part in passed:
            kept = kept + part.astype(jnp.float32)
        kept = kept.astype(jnp.bfloat16).reshape(per_tensor, 2, peers, capacity, depth)
        kept = kept.transpose(2, 0, 1, 3, 4).reshape(peers, -1, depth)
        returned = lax.all_to_all(kept, "dp", split_axis=0, concat_axis=0, tiled=True)
        return returned.reshape(line, 2, 2, per_tensor, 2, capacity, depth)

    own_side = finish(0)
    other_side = finish(1, own_side[0])
    homes = placement.reshape(line, 2, 2, capacity, stored_rows)
    encoded_grad = jnp.einsum(
        "zxckr,zxcpqkd->rpxqd", homes, send_home(*own_side), preferred_element_type=jnp.float32
    ) + jnp.einsum(
        "zxckr,zxcpqkd->rpxqd",
        homes[:, ::-1],
        send_home(*other_side),
        preferred_element_type=jnp.float32,
    )
    return (query_grad, encoded_grad.astype(jnp.bfloat16).reshape(stored_rows, -1))


def solution(mesh):
    in_specs = (
        P("dp", "tensor"),
        P("dp", "tensor"),
        P("dp"),
        P("dp", "tensor"),
        P("dp", None),
        P(None, "dp", "tensor"),
        P(None, "dp", "tensor"),
    )
    out_specs = (P("dp", "tensor"), P("dp", "tensor"))
    return jax.shard_map(
        on_device, mesh=mesh, in_specs=in_specs, out_specs=out_specs, check_vma=False
    )
```

```python
import functools
import math

import jax
import jax.numpy as jnp
from jax import lax
from jax.experimental import pallas as pl
from jax.experimental.pallas import tpu as pltpu
from jax.sharding import PartitionSpec as P

HD = 256
CAP_LIMIT = 10.0
VMEM_LIMIT = 48 * 1024 * 1024


def slot_table(labels, capacity, peer_count):
    targets = (labels[:, None] == jnp.arange(peer_count, dtype=jnp.int32)[None, :]).astype(
        jnp.int32
    )
    before = jnp.cumsum(targets, axis=0) - targets
    rank_in = jnp.sum(before * targets, axis=1)
    slot_index = labels * capacity + rank_in
    placement = jnp.arange(peer_count * capacity, dtype=jnp.int32)[:, None] == slot_index[None, :]
    return placement.astype(jnp.bfloat16)


def split_heads(head_count):
    if head_count < 4:
        return [1] * head_count
    part = (3 * head_count) // 8
    return [head_count - part, part]


def split_units(size):
    return [2] * (size // 2) + [1] * (size % 2)


ANYWHERE = pl.BlockSpec(memory_space=pl.ANY)


def tie_kernel(*refs):
    pass


def tie(value, token):
    return pl.pallas_call(
        tie_kernel,
        in_specs=[ANYWHERE, ANYWHERE],
        out_specs=ANYWHERE,
        out_shape=jax.ShapeDtypeStruct(value.shape, value.dtype),
        input_output_aliases={0: 0},
        cost_estimate=pl.CostEstimate(flops=0, bytes_accessed=0, transcendentals=0),
        name="tie",
    )(value, token)


def predict_kernel(weights, velocity, *rest):
    result = rest[-1]
    for side in range(2):
        result[:, side * HD : (side + 1) * HD] = (
            weights[side].astype(jnp.float32) - velocity[side]
        ).astype(jnp.bfloat16)


def predict_first_kernel(weights, velocity, result, held_weights, held_velocity, held, sems):
    depth = weights.shape[1]
    size = held.shape[0]
    loads, stores = [], []
    for head in range(size):
        at = pl.ds(head * HD, HD)
        loads.append(
            (
                pltpu.make_async_copy(weights.at[:, :, at], held_weights.at[head], sems.at[0, head]),
                pltpu.make_async_copy(
                    velocity.at[:, :, at], held_velocity.at[head], sems.at[1, head]
                ),
            )
        )
        stores.append(
            pltpu.make_async_copy(
                held.at[head], result.at[:, pl.ds(2 * head * HD, 2 * HD)], sems.at[2, head]
            )
        )
        for load in loads[-1]:
            load.start()
    for head in range(size):
        for load in loads[head]:
            load.wait()
        for side in range(2):
            held[head, :, side * HD : (side + 1) * HD] = (
                held_weights[head, side].astype(jnp.float32) - held_velocity[head, side]
            ).astype(jnp.bfloat16)
        stores[head].start()
    for store in stores:
        store.wait()


def predict_first(projections, velocity, size):
    depth = projections.shape[1]
    return pl.pallas_call(
        predict_first_kernel,
        in_specs=[ANYWHERE, ANYWHERE],
        out_specs=ANYWHERE,
        out_shape=jax.ShapeDtypeStruct((depth, 2 * HD * size), jnp.bfloat16),
        scratch_shapes=[
            pltpu.VMEM((size, 2, depth, HD), jnp.bfloat16),
            pltpu.VMEM((size, 2, depth, HD), jnp.float32),
            pltpu.VMEM((size, depth, 2 * HD), jnp.bfloat16),
            pltpu.SemaphoreType.DMA((3, size)),
        ],
        compiler_params=pltpu.CompilerParams(vmem_limit_bytes=VMEM_LIMIT),
        cost_estimate=pl.CostEstimate(
            flops=2 * depth * HD * size, bytes_accessed=16 * depth * HD * size, transcendentals=0
        ),
        name="predict_first",
    )(projections, velocity)


def predict(projections, velocity, first, size, *tokens):
    depth = projections.shape[1]
    if first == 0:
        return predict_first(projections, velocity, size)
    spec = pl.BlockSpec((2, depth, HD), lambda head: (0, 0, first + head))
    return pl.pallas_call(
        predict_kernel,
        grid=(size,),
        in_specs=[spec, spec] + [ANYWHERE] * len(tokens),
        out_specs=pl.BlockSpec((depth, 2 * HD), lambda head: (0, head)),
        out_shape=jax.ShapeDtypeStruct((depth, 2 * HD * size), jnp.bfloat16),
        cost_estimate=pl.CostEstimate(
            flops=2 * depth * HD * size, bytes_accessed=16 * depth * HD * size, transcendentals=0
        ),
        name="predict",
    )(projections, velocity, *tokens)


def arrange_kernel(pos, rows, _, result, *, line, tensor_count):
    per_tensor = line // tensor_count
    slots, depth = rows.shape[3:]
    for x_at in range(2):
        for z in range(line):
            shift = lax.rem(pos[3] - z // per_tensor + tensor_count, tensor_count)
            for core in range(2):
                first = (2 * z + core) * depth
                result[x_at * slots : (x_at + 1) * slots, first : first + depth] = rows[
                    shift * per_tensor + z % per_tensor, core, lax.rem(pos[1] + x_at, 2)
                ]


def arrange(pos, rows, token, line, tensor_count):
    slots, depth = rows.shape[3:]
    return pl.pallas_call(
        functools.partial(arrange_kernel, line=line, tensor_count=tensor_count),
        in_specs=[
            pl.BlockSpec(memory_space=pltpu.SMEM),
            pl.BlockSpec(memory_space=pltpu.VMEM),
            ANYWHERE,
        ],
        out_specs=pl.BlockSpec(memory_space=pltpu.VMEM),
        out_shape=jax.ShapeDtypeStruct((2 * slots, 2 * line * depth), jnp.bfloat16),
        compiler_params=pltpu.CompilerParams(vmem_limit_bytes=VMEM_LIMIT),
        cost_estimate=pl.CostEstimate(
            flops=0, bytes_accessed=4 * rows.size, transcendentals=0
        ),
        name="arrange",
    )(pos, rows, token)


def project_kernel(rows, weights, *rest):
    mine, other = rest[-2:]
    slots = mine.shape[0]
    total = jnp.dot(rows[...], weights[...], preferred_element_type=jnp.float32)
    mine[...] = total[:slots]
    other[...] = total[slots:].astype(other.dtype)


def project(rows, weights, first, width, *tokens):
    features = weights.shape[0]
    first_block = first // HD
    slots = rows.shape[0] // 2
    result_spec = pl.BlockSpec((slots, HD), lambda at: (0, at))
    return pl.pallas_call(
        project_kernel,
        grid=(width // HD,),
        in_specs=[
            pl.BlockSpec(rows.shape, lambda at: (0, 0)),
            pl.BlockSpec((features, HD), lambda at: (0, first_block + at)),
        ]
        + [ANYWHERE] * len(tokens),
        out_specs=[result_spec, result_spec],
        out_shape=(
            jax.ShapeDtypeStruct((slots, width), jnp.float32),
            jax.ShapeDtypeStruct((slots, width), jnp.bfloat16),
        ),
        compiler_params=pltpu.CompilerParams(vmem_limit_bytes=VMEM_LIMIT),
        cost_estimate=pl.CostEstimate(
            flops=2 * 2 * slots * features * width,
            bytes_accessed=2 * features * width + rows.size * 2 + 6 * slots * width,
            transcendentals=0,
        ),
        name="project",
    )(rows, weights, *tokens)


def attend_kernel(block, live, usable, queries, grads, mine, received, *rest):
    query_grad, pair_grad, key_total, value_total = rest[-4:]
    both = (mine[...] + received[...].astype(jnp.float32)).astype(jnp.bfloat16)
    keys, values = both[:, :HD], both[:, HD:]
    scale = 1.0 / math.sqrt(HD)
    mask = usable[...]
    last_dims = (((1,), (1,)), ((), ()))
    query_count = queries.shape[0]
    for first in range(0, query_count, block):
        at = pl.ds(first, block)
        q = queries[at, :]
        position = first + lax.broadcasted_iota(jnp.int32, (block, 1), 0)
        g = grads[at, :]
        g = jnp.where(position < live[0], g, jnp.zeros_like(g))
        raw = lax.dot_general(keys, q, last_dims, preferred_element_type=jnp.float32)
        bent = jnp.tanh(raw * (scale / CAP_LIMIT))
        terms = jnp.exp(bent * CAP_LIMIT) * mask
        attention = terms * (1.0 / jnp.sum(terms, axis=0, keepdims=True))
        prob_grad = lax.dot_general(values, g, last_dims, preferred_element_type=jnp.float32)
        row_term = jnp.sum(attention * prob_grad, axis=0, keepdims=True)
        score_grad = (
            attention * (prob_grad - row_term) * ((1.0 - bent * bent) * scale)
        ).astype(jnp.bfloat16)
        rounded = attention.astype(jnp.bfloat16)
        query_grad[at, :] = lax.dot_general(
            score_grad, keys, (((0,), (0,)), ((), ())), preferred_element_type=jnp.float32
        ).astype(jnp.bfloat16)
        key_block = jnp.dot(score_grad, q, preferred_element_type=jnp.float32)
        value_block = jnp.dot(rounded, g, preferred_element_type=jnp.float32)
        if first == 0:
            key_total[...] = key_block
            value_total[...] = value_block
        else:
            key_total[...] += key_block
            value_total[...] += value_block
    pair_grad[:, :HD] = key_total[...].astype(jnp.bfloat16)
    pair_grad[:, HD:] = value_total[...].astype(jnp.bfloat16)


def attend(live, usable, queries, grads, mine, received, first_head, earlier, *tokens):
    query_count, width = queries.shape
    slots, chunk = mine.shape
    heads = chunk // (2 * HD)
    block = min(1024, query_count)
    columns = pl.BlockSpec((query_count, HD), lambda head: (0, first_head + head))
    pair = pl.BlockSpec((slots, 2 * HD), lambda head: (0, head))
    operands = [live, usable, queries, grads, mine, received]
    in_specs = [
        pl.BlockSpec(memory_space=pltpu.SMEM),
        pl.BlockSpec((slots, 1), lambda head: (0, 0)),
        columns,
        columns,
        pair,
        pair,
    ]
    aliases = {}
    if earlier is not None:
        aliases = {len(operands): 0}
        operands.append(earlier)
        in_specs.append(ANYWHERE)
    operands += tokens
    in_specs += [ANYWHERE] * len(tokens)
    return pl.pallas_call(
        functools.partial(attend_kernel, block),
        grid=(heads,),
        in_specs=in_specs,
        out_specs=[columns, pair],
        out_shape=(
            jax.ShapeDtypeStruct((query_count, width), jnp.bfloat16),
            jax.ShapeDtypeStruct((slots, chunk), jnp.bfloat16),
        ),
        scratch_shapes=[pltpu.VMEM((slots, HD), jnp.float32)] * 2,
        input_output_aliases=aliases,
        compiler_params=pltpu.CompilerParams(vmem_limit_bytes=VMEM_LIMIT),
        cost_estimate=pl.CostEstimate(
            flops=5 * query_count * slots * chunk,
            bytes_accessed=3 * query_count * chunk + 10 * slots * chunk,
            transcendentals=2 * query_count * slots * heads,
        ),
        name="attend",
    )(*operands)


def spread_kernel(pos, *refs, parts, sides, earlier):
    scratch = parts if len(sides) > 1 else 0
    result, joined = refs[len(refs) - 1 - scratch], refs[len(refs) - scratch :]
    stride = len(sides) + 1
    depth = result.shape[-1]
    slots = refs[0].shape[0]

    if scratch:

        @pl.when(pl.program_id(0) == 0)
        def _():
            for part in range(parts):
                for at in range(len(sides)):
                    joined[part][at * slots : (at + 1) * slots] = refs[stride * part + at][...]

    total = None
    for part in range(parts):
        grads = joined[part] if scratch else refs[stride * part]
        term = lax.dot_general(
            grads[...],
            refs[stride * part + stride - 1][...],
            (((1,), (1,)), ((), ())),
            preferred_element_type=jnp.float32,
        )
        total = term if total is None else total + term
    for core in range(2):
        for at in range(len(sides)):
            share = total[at * slots : (at + 1) * slots, core * depth : (core + 1) * depth]
            if earlier:
                share = share + refs[stride * parts][0, core, at]
            result[0, core, at] = share.astype(result.dtype)


def spread(pos, depth, units, earlier, sides, first, count, tensor_count, dtype, *tokens):
    line = units[0][2].shape[0] // (2 * depth)
    slots = units[0][0].shape[0]
    per_tensor = line // tensor_count

    def weight_at(column):
        def index(step, pos):
            block = first + step
            return (
                lax.rem(pos[3] + block // per_tensor, tensor_count) * per_tensor
                + lax.rem(block, per_tensor),
                column,
            )

        return index

    operands, in_specs, scratch, widths = [pos], [], [], 0
    for unit in units:
        width = unit[0].shape[1]
        for side in sides:
            operands.append(unit[side])
            in_specs.append(pl.BlockSpec((slots, width), lambda step, pos: (0, 0)))
        operands.append(unit[2])
        in_specs.append(pl.BlockSpec((2 * depth, width), weight_at(unit[3] // width)))
        if len(sides) > 1:
            scratch.append(pltpu.VMEM((len(sides) * slots, width), jnp.bfloat16))
        widths += width
    block = (1, 2, len(sides), slots, depth)
    if earlier is not None:
        operands.append(earlier)
        side = sides[0] if len(sides) == 1 else 0
        in_specs.append(pl.BlockSpec(block, lambda step, pos: (first + step, 0, side, 0, 0)))
    operands += tokens
    in_specs += [ANYWHERE] * len(tokens)
    return pl.pallas_call(
        functools.partial(
            spread_kernel, parts=len(units), sides=sides, earlier=earlier is not None
        ),
        grid_spec=pltpu.PrefetchScalarGridSpec(
            num_scalar_prefetch=1,
            grid=(count,),
            in_specs=in_specs,
            out_specs=pl.BlockSpec(block, lambda step, pos: (step, 0, 0, 0, 0)),
            scratch_shapes=scratch,
        ),
        out_shape=jax.ShapeDtypeStruct((count,) + block[1:], dtype),
        compiler_params=pltpu.CompilerParams(vmem_limit_bytes=VMEM_LIMIT),
        cost_estimate=pl.CostEstimate(
            flops=2 * len(sides) * slots * 2 * count * depth * widths,
            bytes_accessed=4 * count * depth * widths + 8 * count * math.prod(block),
            transcendentals=0,
        ),
        name="spread",
    )(*operands)


def on_device(queries, out_grad, target_len, encoded, row_owner, projections, velocity):
    peers = lax.axis_size("dp")
    tensor_count = lax.axis_size("tensor")
    line = peers // 4
    per_tensor = line // tensor_count
    stored_rows = encoded.shape[0]
    depth = projections.shape[1]
    capacity = max(2, 2 * stored_rows // peers)
    slots = peers * capacity
    place = lax.axis_index("dp")
    tensor_at = lax.axis_index("tensor")
    pos = jnp.stack([place // 4, (place // 2) % 2, place % 2, tensor_at]).astype(jnp.int32)
    columns = [[i for i in range(peers) if (i // 2) % 2 == side] for side in range(2)]
    x_swap = [(i, i ^ 2) for i in range(peers)]

    def tensor_shift(value, shift):
        pairs = [(i, (i + shift) % tensor_count) for i in range(tensor_count)]
        return lax.ppermute(value, "tensor", pairs)

    placement = slot_table(row_owner[:, 0], capacity, peers)
    filled = jnp.sum(placement.astype(jnp.float32), axis=1).astype(jnp.bfloat16)
    outgoing = jnp.dot(placement, encoded, preferred_element_type=jnp.float32).astype(jnp.bfloat16)
    outgoing = outgoing.reshape(line, 2, 2, capacity, per_tensor, 2, 2, depth)
    outgoing = outgoing.transpose(0, 5, 2, 4, 6, 1, 3, 7).reshape(peers, -1, depth)

    incoming = lax.all_to_all(outgoing, "dp", split_axis=0, concat_axis=0, tiled=True)
    parts = []
    first, token = 0, ()
    for size in split_heads(queries.shape[1] // HD):
        block = predict(projections, velocity, first, size, *token)
        gathered = lax.all_gather(block, "dp", axis=0, tiled=True, axis_index_groups=columns)
        parts.append((first, size, gathered))
        first, token = first + size, (block, incoming)

    usable = lax.all_to_all(filled, "dp", split_axis=0, concat_axis=0, tiled=True)
    usable = (usable.astype(jnp.float32) > 0.5).astype(jnp.float32)[:, None]
    incoming = incoming.reshape(peers, per_tensor, 2, 2, capacity, depth)
    incoming = incoming.transpose(1, 2, 3, 0, 4, 5).reshape(per_tensor, 2, 2, slots, depth)
    rows = jnp.concatenate(
        [incoming] + [tensor_shift(incoming, shift) for shift in range(1, tensor_count)]
    )
    rows = arrange(pos, rows, usable, line, tensor_count)

    query_grad, token, units, early, exchanged = None, (), [], None, []
    for at, (first, size, weights) in enumerate(parts):
        final = at == len(parts) - 1
        if final:
            early = spread(
                pos, depth, units, None, (0, 1), 0, line, tensor_count, jnp.float32
            )
            units = []
        products, column = [], 0
        for heads in split_units(size):
            width = 2 * HD * heads
            mine, other = project(rows, weights, column, width, *token)
            products.append((column, mine, lax.ppermute(other, "dp", x_swap)))
            column += width
        for column, mine, received in products:
            query_grad, pair_grad = attend(
                target_len,
                usable,
                queries,
                out_grad,
                mine,
                received,
                first + column // (2 * HD),
                query_grad,
                *((early,) if final else ()),
                *exchanged[-2:-1],
            )
            exchanged.append(lax.ppermute(pair_grad, "dp", x_swap))
            units.append((pair_grad, exchanged[-1], weights, column))
            token = (pair_grad,)

    sent, passed, kept = [], [], []
    for side in range(2):
        sent.append(
            spread(
                pos, depth, units, early, (side,), per_tensor, line - per_tensor, tensor_count,
                jnp.bfloat16, *sent,
            )
        )
        passed.append(
            [
                tensor_shift(sent[side][(shift - 1) * per_tensor : shift * per_tensor], shift)
                for shift in range(1, tensor_count)
            ]
        )
    for side in range(2):
        kept.append(
            spread(
                pos, depth, units, early, (side,), 0, per_tensor, tensor_count, jnp.float32,
                sent[side], *kept,
            )
        )
    passed[0] = [tie(part, sent[1]) for part in passed[0]]

    def send_home(kept, passed):
        for part in passed:
            kept = kept + part.astype(jnp.float32)
        kept = kept.astype(jnp.bfloat16).reshape(per_tensor, 2, peers, capacity, depth)
        kept = kept.transpose(2, 0, 1, 3, 4).reshape(peers, -1, depth)
        returned = lax.all_to_all(kept, "dp", split_axis=0, concat_axis=0, tiled=True)
        return returned.reshape(line, 2, 2, per_tensor, 2, capacity, depth)

    homes = placement.reshape(line, 2, 2, capacity, stored_rows)
    encoded_grad = jnp.einsum(
        "zxckr,zxcpqkd->rpxqd", homes, send_home(kept[0], passed[0]), preferred_element_type=jnp.float32
    ) + jnp.einsum(
        "zxckr,zxcpqkd->rpxqd",
        homes[:, ::-1],
        send_home(kept[1], passed[1]),
        preferred_element_type=jnp.float32,
    )
    return (query_grad, encoded_grad.astype(jnp.bfloat16).reshape(stored_rows, -1))


def solution(mesh):
    in_specs = (
        P("dp", "tensor"),
        P("dp", "tensor"),
        P("dp"),
        P("dp", "tensor"),
        P("dp", None),
        P(None, "dp", "tensor"),
        P(None, "dp", "tensor"),
    )
    out_specs = (P("dp", "tensor"), P("dp", "tensor"))
    return jax.shard_map(
        on_device, mesh=mesh, in_specs=in_specs, out_specs=out_specs, check_vma=False
    )
```

```python
import functools
import math

import jax
import jax.numpy as jnp
from jax import lax
from jax.experimental import pallas as pl
from jax.experimental.pallas import tpu as pltpu
from jax.sharding import PartitionSpec as P

HD = 256
CAP_LIMIT = 10.0
VMEM_LIMIT = 48 * 1024 * 1024
VMEM_WHOLE = 60 * 1024 * 1024


def slot_table(labels, capacity, peer_count):
    targets = (labels[:, None] == jnp.arange(peer_count, dtype=jnp.int32)[None, :]).astype(
        jnp.int32
    )
    before = jnp.cumsum(targets, axis=0) - targets
    rank_in = jnp.sum(before * targets, axis=1)
    slot_index = labels * capacity + rank_in
    placement = jnp.arange(peer_count * capacity, dtype=jnp.int32)[:, None] == slot_index[None, :]
    return placement.astype(jnp.bfloat16)


def split_heads(head_count):
    if head_count < 4:
        return [1] * head_count
    part = (3 * head_count) // 8
    return [head_count - part, part]


def split_units(size):
    return [2] * (size // 2) + [1] * (size % 2)


ANYWHERE = pl.BlockSpec(memory_space=pl.ANY)


def tie_kernel(*refs):
    pass


def tie(value, token):
    return pl.pallas_call(
        tie_kernel,
        in_specs=[ANYWHERE, ANYWHERE],
        out_specs=ANYWHERE,
        out_shape=jax.ShapeDtypeStruct(value.shape, value.dtype),
        input_output_aliases={0: 0},
        cost_estimate=pl.CostEstimate(flops=0, bytes_accessed=0, transcendentals=0),
        name="tie",
    )(value, token)


def predict_kernel(weights, velocity, *rest):
    result = rest[-1]
    for side in range(2):
        result[:, side * HD : (side + 1) * HD] = (
            weights[side].astype(jnp.float32) - velocity[side]
        ).astype(jnp.bfloat16)


def predict_first_kernel(weights, velocity, result, held_weights, held_velocity, held, sems):
    depth = weights.shape[1]
    size = held.shape[0]
    loads, stores = [], []
    for head in range(size):
        at = pl.ds(head * HD, HD)
        loads.append(
            (
                pltpu.make_async_copy(weights.at[:, :, at], held_weights.at[head], sems.at[0, head]),
                pltpu.make_async_copy(
                    velocity.at[:, :, at], held_velocity.at[head], sems.at[1, head]
                ),
            )
        )
        stores.append(
            pltpu.make_async_copy(
                held.at[head], result.at[:, pl.ds(2 * head * HD, 2 * HD)], sems.at[2, head]
            )
        )
        for load in loads[-1]:
            load.start()
    for head in range(size):
        for load in loads[head]:
            load.wait()
        for side in range(2):
            held[head, :, side * HD : (side + 1) * HD] = (
                held_weights[head, side].astype(jnp.float32) - held_velocity[head, side]
            ).astype(jnp.bfloat16)
        stores[head].start()
    for store in stores:
        store.wait()


def predict_first(projections, velocity, size):
    depth = projections.shape[1]
    return pl.pallas_call(
        predict_first_kernel,
        in_specs=[ANYWHERE, ANYWHERE],
        out_specs=ANYWHERE,
        out_shape=jax.ShapeDtypeStruct((depth, 2 * HD * size), jnp.bfloat16),
        scratch_shapes=[
            pltpu.VMEM((size, 2, depth, HD), jnp.bfloat16),
            pltpu.VMEM((size, 2, depth, HD), jnp.float32),
            pltpu.VMEM((size, depth, 2 * HD), jnp.bfloat16),
            pltpu.SemaphoreType.DMA((3, size)),
        ],
        compiler_params=pltpu.CompilerParams(vmem_limit_bytes=VMEM_WHOLE),
        cost_estimate=pl.CostEstimate(
            flops=2 * depth * HD * size, bytes_accessed=16 * depth * HD * size, transcendentals=0
        ),
        name="predict_first",
    )(projections, velocity)


def predict(projections, velocity, first, size, *tokens):
    depth = projections.shape[1]
    if first == 0:
        return predict_first(projections, velocity, size)
    spec = pl.BlockSpec((2, depth, HD), lambda head: (0, 0, first + head))
    return pl.pallas_call(
        predict_kernel,
        grid=(size,),
        in_specs=[spec, spec] + [ANYWHERE] * len(tokens),
        out_specs=pl.BlockSpec((depth, 2 * HD), lambda head: (0, head)),
        out_shape=jax.ShapeDtypeStruct((depth, 2 * HD * size), jnp.bfloat16),
        cost_estimate=pl.CostEstimate(
            flops=2 * depth * HD * size, bytes_accessed=16 * depth * HD * size, transcendentals=0
        ),
        name="predict",
    )(projections, velocity, *tokens)


def arrange_kernel(pos, rows, _, result, *, line, tensor_count):
    per_tensor = line // tensor_count
    slots, depth = rows.shape[3:]
    for x_at in range(2):
        for z in range(line):
            shift = lax.rem(pos[3] - z // per_tensor + tensor_count, tensor_count)
            for core in range(2):
                first = (2 * z + core) * depth
                result[x_at * slots : (x_at + 1) * slots, first : first + depth] = rows[
                    shift * per_tensor + z % per_tensor, core, lax.rem(pos[1] + x_at, 2)
                ]


def arrange(pos, rows, token, line, tensor_count):
    slots, depth = rows.shape[3:]
    return pl.pallas_call(
        functools.partial(arrange_kernel, line=line, tensor_count=tensor_count),
        in_specs=[
            pl.BlockSpec(memory_space=pltpu.SMEM),
            pl.BlockSpec(memory_space=pltpu.VMEM),
            ANYWHERE,
        ],
        out_specs=pl.BlockSpec(memory_space=pltpu.VMEM),
        out_shape=jax.ShapeDtypeStruct((2 * slots, 2 * line * depth), jnp.bfloat16),
        compiler_params=pltpu.CompilerParams(vmem_limit_bytes=VMEM_LIMIT),
        cost_estimate=pl.CostEstimate(
            flops=0, bytes_accessed=4 * rows.size, transcendentals=0
        ),
        name="arrange",
    )(pos, rows, token)


def project_kernel(rows, weights, *rest):
    mine, other = rest[-2:]
    slots = mine.shape[0]
    total = jnp.dot(rows[...], weights[...], preferred_element_type=jnp.float32)
    mine[...] = total[:slots]
    other[...] = total[slots:].astype(other.dtype)


def project(rows, weights, first, width, *tokens):
    features = weights.shape[0]
    first_block = first // HD
    slots = rows.shape[0] // 2
    result_spec = pl.BlockSpec((slots, HD), lambda at: (0, at))
    return pl.pallas_call(
        project_kernel,
        grid=(width // HD,),
        in_specs=[
            pl.BlockSpec(rows.shape, lambda at: (0, 0)),
            pl.BlockSpec((features, HD), lambda at: (0, first_block + at)),
        ]
        + [ANYWHERE] * len(tokens),
        out_specs=[result_spec, result_spec],
        out_shape=(
            jax.ShapeDtypeStruct((slots, width), jnp.float32),
            jax.ShapeDtypeStruct((slots, width), jnp.bfloat16),
        ),
        compiler_params=pltpu.CompilerParams(vmem_limit_bytes=VMEM_LIMIT),
        cost_estimate=pl.CostEstimate(
            flops=2 * 2 * slots * features * width,
            bytes_accessed=2 * features * width + rows.size * 2 + 6 * slots * width,
            transcendentals=0,
        ),
        name="project",
    )(rows, weights, *tokens)


def attend_kernel(block, live, usable, queries, grads, mine, received, *rest):
    query_grad, pair_grad, key_total, value_total = rest[-4:]
    both = (mine[...] + received[...].astype(jnp.float32)).astype(jnp.bfloat16)
    keys, values = both[:, :HD], both[:, HD:]
    scale = 1.0 / math.sqrt(HD)
    mask = usable[...]
    last_dims = (((1,), (1,)), ((), ()))
    query_count = queries.shape[0]
    for first in range(0, query_count, block):
        at = pl.ds(first, block)
        q = queries[at, :]
        position = first + lax.broadcasted_iota(jnp.int32, (block, 1), 0)
        g = grads[at, :]
        g = jnp.where(position < live[0], g, jnp.zeros_like(g))
        raw = lax.dot_general(keys, q, last_dims, preferred_element_type=jnp.float32)
        bent = jnp.tanh(raw * (scale / CAP_LIMIT))
        terms = jnp.exp(bent * CAP_LIMIT) * mask
        attention = terms * (1.0 / jnp.sum(terms, axis=0, keepdims=True))
        prob_grad = lax.dot_general(values, g, last_dims, preferred_element_type=jnp.float32)
        row_term = jnp.sum(attention * prob_grad, axis=0, keepdims=True)
        score_grad = (
            attention * (prob_grad - row_term) * ((1.0 - bent * bent) * scale)
        ).astype(jnp.bfloat16)
        rounded = attention.astype(jnp.bfloat16)
        query_grad[at, :] = lax.dot_general(
            score_grad, keys, (((0,), (0,)), ((), ())), preferred_element_type=jnp.float32
        ).astype(jnp.bfloat16)
        key_block = jnp.dot(score_grad, q, preferred_element_type=jnp.float32)
        value_block = jnp.dot(rounded, g, preferred_element_type=jnp.float32)
        if first == 0:
            key_total[...] = key_block
            value_total[...] = value_block
        else:
            key_total[...] += key_block
            value_total[...] += value_block
    pair_grad[:, :HD] = key_total[...].astype(jnp.bfloat16)
    pair_grad[:, HD:] = value_total[...].astype(jnp.bfloat16)


def attend(live, usable, queries, grads, mine, received, first_head, earlier, *tokens):
    query_count, width = queries.shape
    slots, chunk = mine.shape
    heads = chunk // (2 * HD)
    block = min(1024, query_count)
    columns = pl.BlockSpec((query_count, HD), lambda head: (0, first_head + head))
    pair = pl.BlockSpec((slots, 2 * HD), lambda head: (0, head))
    operands = [live, usable, queries, grads, mine, received]
    in_specs = [
        pl.BlockSpec(memory_space=pltpu.SMEM),
        pl.BlockSpec((slots, 1), lambda head: (0, 0)),
        columns,
        columns,
        pair,
        pair,
    ]
    aliases = {}
    if earlier is not None:
        aliases = {len(operands): 0}
        operands.append(earlier)
        in_specs.append(ANYWHERE)
    operands += tokens
    in_specs += [ANYWHERE] * len(tokens)
    return pl.pallas_call(
        functools.partial(attend_kernel, block),
        grid=(heads,),
        in_specs=in_specs,
        out_specs=[columns, pair],
        out_shape=(
            jax.ShapeDtypeStruct((query_count, width), jnp.bfloat16),
            jax.ShapeDtypeStruct((slots, chunk), jnp.bfloat16),
        ),
        scratch_shapes=[pltpu.VMEM((slots, HD), jnp.float32)] * 2,
        input_output_aliases=aliases,
        compiler_params=pltpu.CompilerParams(vmem_limit_bytes=VMEM_LIMIT),
        cost_estimate=pl.CostEstimate(
            flops=5 * query_count * slots * chunk,
            bytes_accessed=3 * query_count * chunk + 10 * slots * chunk,
            transcendentals=2 * query_count * slots * heads,
        ),
        name="attend",
    )(*operands)


def spread_kernel(pos, *refs, parts, sides, earlier):
    scratch = parts if len(sides) > 1 else 0
    result, mark = refs[len(refs) - 2 - scratch : len(refs) - scratch]
    joined = refs[len(refs) - scratch :]
    mark[...] = jnp.zeros_like(mark)
    stride = len(sides) + 1
    depth = result.shape[-1]
    slots = refs[0].shape[0]

    if scratch:

        @pl.when(pl.program_id(0) == 0)
        def _():
            for part in range(parts):
                for at in range(len(sides)):
                    joined[part][at * slots : (at + 1) * slots] = refs[stride * part + at][...]

    total = None
    for part in range(parts):
        grads = joined[part] if scratch else refs[stride * part]
        term = lax.dot_general(
            grads[...],
            refs[stride * part + stride - 1][...],
            (((1,), (1,)), ((), ())),
            preferred_element_type=jnp.float32,
        )
        total = term if total is None else total + term
    for core in range(2):
        for at in range(len(sides)):
            share = total[at * slots : (at + 1) * slots, core * depth : (core + 1) * depth]
            if earlier:
                share = share + refs[stride * parts][0, core, at]
            result[0, core, at] = share.astype(result.dtype)


def spread(pos, depth, units, earlier, sides, first, count, tensor_count, dtype, *tokens):
    line = units[0][2].shape[0] // (2 * depth)
    slots = units[0][0].shape[0]
    per_tensor = line // tensor_count

    def weight_at(column):
        def index(step, pos):
            block = first + step
            return (
                lax.rem(pos[3] + block // per_tensor, tensor_count) * per_tensor
                + lax.rem(block, per_tensor),
                column,
            )

        return index

    operands, in_specs, scratch, widths = [pos], [], [], 0
    for unit in units:
        width = unit[0].shape[1]
        for side in sides:
            operands.append(unit[side])
            in_specs.append(pl.BlockSpec((slots, width), lambda step, pos: (0, 0)))
        operands.append(unit[2])
        in_specs.append(pl.BlockSpec((2 * depth, width), weight_at(unit[3] // width)))
        if len(sides) > 1:
            scratch.append(pltpu.VMEM((len(sides) * slots, width), jnp.bfloat16))
        widths += width
    block = (1, 2, len(sides), slots, depth)
    if earlier is not None:
        operands.append(earlier)
        side = sides[0] if len(sides) == 1 else 0
        in_specs.append(pl.BlockSpec(block, lambda step, pos: (first + step, 0, side, 0, 0)))
    operands += tokens
    in_specs += [ANYWHERE] * len(tokens)
    return pl.pallas_call(
        functools.partial(
            spread_kernel, parts=len(units), sides=sides, earlier=earlier is not None
        ),
        grid_spec=pltpu.PrefetchScalarGridSpec(
            num_scalar_prefetch=1,
            grid=(count,),
            in_specs=in_specs,
            out_specs=[
                pl.BlockSpec(block, lambda step, pos: (step, 0, 0, 0, 0)),
                pl.BlockSpec((8, 128), lambda step, pos: (0, 0)),
            ],
            scratch_shapes=scratch,
        ),
        out_shape=(
            jax.ShapeDtypeStruct((count,) + block[1:], dtype),
            jax.ShapeDtypeStruct((8, 128), jnp.float32),
        ),
        compiler_params=pltpu.CompilerParams(vmem_limit_bytes=VMEM_LIMIT),
        cost_estimate=pl.CostEstimate(
            flops=2 * len(sides) * slots * 2 * count * depth * widths,
            bytes_accessed=4 * count * depth * widths + 8 * count * math.prod(block),
            transcendentals=0,
        ),
        name="spread",
    )(*operands)


def on_device(queries, out_grad, target_len, encoded, row_owner, projections, velocity):
    peers = lax.axis_size("dp")
    tensor_count = lax.axis_size("tensor")
    line = peers // 4
    per_tensor = line // tensor_count
    stored_rows = encoded.shape[0]
    depth = projections.shape[1]
    capacity = max(2, 2 * stored_rows // peers)
    slots = peers * capacity
    place = lax.axis_index("dp")
    tensor_at = lax.axis_index("tensor")
    pos = jnp.stack([place // 4, (place // 2) % 2, place % 2, tensor_at]).astype(jnp.int32)
    columns = [[i for i in range(peers) if (i // 2) % 2 == side] for side in range(2)]
    x_swap = [(i, i ^ 2) for i in range(peers)]

    def tensor_shift(value, shift):
        pairs = [(i, (i + shift) % tensor_count) for i in range(tensor_count)]
        return lax.ppermute(value, "tensor", pairs)

    placement = slot_table(row_owner[:, 0], capacity, peers)
    filled = jnp.sum(placement.astype(jnp.float32), axis=1).astype(jnp.bfloat16)
    outgoing = jnp.dot(placement, encoded, preferred_element_type=jnp.float32).astype(jnp.bfloat16)
    outgoing = outgoing.reshape(line, 2, 2, capacity, per_tensor, 2, 2, depth)
    outgoing = outgoing.transpose(0, 5, 2, 4, 6, 1, 3, 7).reshape(peers, -1, depth)

    incoming = lax.all_to_all(outgoing, "dp", split_axis=0, concat_axis=0, tiled=True)
    parts = []
    first, token = 0, ()
    for size in split_heads(queries.shape[1] // HD):
        block = predict(projections, velocity, first, size, *token)
        gathered = lax.all_gather(block, "dp", axis=0, tiled=True, axis_index_groups=columns)
        parts.append((first, size, gathered))
        first, token = first + size, (block, incoming)

    usable = lax.all_to_all(filled, "dp", split_axis=0, concat_axis=0, tiled=True)
    usable = (usable.astype(jnp.float32) > 0.5).astype(jnp.float32)[:, None]
    incoming = incoming.reshape(peers, per_tensor, 2, 2, capacity, depth)
    incoming = incoming.transpose(1, 2, 3, 0, 4, 5).reshape(per_tensor, 2, 2, slots, depth)
    rows = jnp.concatenate(
        [incoming] + [tensor_shift(incoming, shift) for shift in range(1, tensor_count)]
    )
    rows = arrange(pos, rows, usable, line, tensor_count)

    query_grad, token, units, early, exchanged = None, (), [], None, []
    for at, (first, size, weights) in enumerate(parts):
        final = at == len(parts) - 1
        if final:
            early, done = spread(
                pos, depth, units, None, (0, 1), 0, line, tensor_count, jnp.float32
            )
            units = []
        products, column = [], 0
        for heads in split_units(size):
            width = 2 * HD * heads
            mine, other = project(rows, weights, column, width, *token)
            products.append((column, mine, lax.ppermute(other, "dp", x_swap)))
            column += width
        for column, mine, received in products:
            query_grad, pair_grad = attend(
                target_len,
                usable,
                queries,
                out_grad,
                mine,
                received,
                first + column // (2 * HD),
                query_grad,
                *((done,) if final else ()),
                *exchanged[-2:-1],
            )
            exchanged.append(lax.ppermute(pair_grad, "dp", x_swap))
            units.append((pair_grad, exchanged[-1], weights, column))
            token = (pair_grad,)

    passed, kept, marks = [], [], []
    for side in range(2):
        sent, mark = spread(
            pos, depth, units, early, (side,), per_tensor, line - per_tensor, tensor_count,
            jnp.bfloat16, *marks,
        )
        marks.append(mark)
        passed.append(
            [
                tensor_shift(sent[(shift - 1) * per_tensor : shift * per_tensor], shift)
                for shift in range(1, tensor_count)
            ]
        )
    for side in range(2):
        kept.append(
            spread(
                pos, depth, units, early, (side,), 0, per_tensor, tensor_count, jnp.float32,
                marks[side],
            )[0]
        )
    kept[0] = tie(kept[0], marks[1])

    def send_home(kept, passed):
        for part in passed:
            kept = kept + part.astype(jnp.float32)
        kept = kept.astype(jnp.bfloat16).reshape(per_tensor, 2, peers, capacity, depth)
        kept = kept.transpose(2, 0, 1, 3, 4).reshape(peers, -1, depth)
        returned = lax.all_to_all(kept, "dp", split_axis=0, concat_axis=0, tiled=True)
        return returned.reshape(line, 2, 2, per_tensor, 2, capacity, depth)

    homes = placement.reshape(line, 2, 2, capacity, stored_rows)
    encoded_grad = jnp.einsum(
        "zxckr,zxcpqkd->rpxqd", homes, send_home(kept[0], passed[0]), preferred_element_type=jnp.float32
    ) + jnp.einsum(
        "zxckr,zxcpqkd->rpxqd",
        homes[:, ::-1],
        send_home(kept[1], passed[1]),
        preferred_element_type=jnp.float32,
    )
    return (query_grad, encoded_grad.astype(jnp.bfloat16).reshape(stored_rows, -1))


def solution(mesh):
    in_specs = (
        P("dp", "tensor"),
        P("dp", "tensor"),
        P("dp"),
        P("dp", "tensor"),
        P("dp", None),
        P(None, "dp", "tensor"),
        P(None, "dp", "tensor"),
    )
    out_specs = (P("dp", "tensor"), P("dp", "tensor"))
    return jax.shard_map(
        on_device, mesh=mesh, in_specs=in_specs, out_specs=out_specs, check_vma=False
    )
```

```python
import functools
import math

import jax
import jax.numpy as jnp
from jax import lax
from jax.experimental import pallas as pl
from jax.experimental.pallas import tpu as pltpu
from jax.sharding import PartitionSpec as P

HD = 256
CAP_LIMIT = 10.0
VMEM_LIMIT = 48 * 1024 * 1024
VMEM_WHOLE = 60 * 1024 * 1024


def slot_table(labels, capacity, peer_count):
    targets = (labels[:, None] == jnp.arange(peer_count, dtype=jnp.int32)[None, :]).astype(
        jnp.int32
    )
    before = jnp.cumsum(targets, axis=0) - targets
    rank_in = jnp.sum(before * targets, axis=1)
    slot_index = labels * capacity + rank_in
    placement = jnp.arange(peer_count * capacity, dtype=jnp.int32)[:, None] == slot_index[None, :]
    return placement.astype(jnp.bfloat16)


def split_heads(head_count):
    if head_count < 4:
        return [1] * head_count
    part = (3 * head_count) // 8
    return [head_count - part, part]


def split_units(size):
    return [2] * (size // 2) + [1] * (size % 2)


ANYWHERE = pl.BlockSpec(memory_space=pl.ANY)


def tie_kernel(*refs):
    pass


def tie(value, token):
    return pl.pallas_call(
        tie_kernel,
        in_specs=[ANYWHERE, ANYWHERE],
        out_specs=ANYWHERE,
        out_shape=jax.ShapeDtypeStruct(value.shape, value.dtype),
        input_output_aliases={0: 0},
        cost_estimate=pl.CostEstimate(flops=0, bytes_accessed=0, transcendentals=0),
        name="tie",
    )(value, token)


def predict_kernel(weights, velocity, *rest):
    result = rest[-1]
    for side in range(2):
        result[:, side * HD : (side + 1) * HD] = (
            weights[side].astype(jnp.float32) - velocity[side]
        ).astype(jnp.bfloat16)


def predict_first_kernel(weights, velocity, result, held_weights, held_velocity, held, sems):
    depth = weights.shape[1]
    size = held.shape[0]
    loads, stores = [], []
    for head in range(size):
        at = pl.ds(head * HD, HD)
        loads.append(
            (
                pltpu.make_async_copy(weights.at[:, :, at], held_weights.at[head], sems.at[0, head]),
                pltpu.make_async_copy(
                    velocity.at[:, :, at], held_velocity.at[head], sems.at[1, head]
                ),
            )
        )
        stores.append(
            pltpu.make_async_copy(
                held.at[head], result.at[:, pl.ds(2 * head * HD, 2 * HD)], sems.at[2, head]
            )
        )
        for load in loads[-1]:
            load.start()
    for head in range(size):
        for load in loads[head]:
            load.wait()
        for side in range(2):
            held[head, :, side * HD : (side + 1) * HD] = (
                held_weights[head, side].astype(jnp.float32) - held_velocity[head, side]
            ).astype(jnp.bfloat16)
        stores[head].start()
    for store in stores:
        store.wait()


def predict_first(projections, velocity, size):
    depth = projections.shape[1]
    return pl.pallas_call(
        predict_first_kernel,
        in_specs=[ANYWHERE, ANYWHERE],
        out_specs=ANYWHERE,
        out_shape=jax.ShapeDtypeStruct((depth, 2 * HD * size), jnp.bfloat16),
        scratch_shapes=[
            pltpu.VMEM((size, 2, depth, HD), jnp.bfloat16),
            pltpu.VMEM((size, 2, depth, HD), jnp.float32),
            pltpu.VMEM((size, depth, 2 * HD), jnp.bfloat16),
            pltpu.SemaphoreType.DMA((3, size)),
        ],
        compiler_params=pltpu.CompilerParams(vmem_limit_bytes=VMEM_WHOLE),
        cost_estimate=pl.CostEstimate(
            flops=2 * depth * HD * size, bytes_accessed=16 * depth * HD * size, transcendentals=0
        ),
        name="predict_first",
    )(projections, velocity)


def predict(projections, velocity, first, size, *tokens):
    depth = projections.shape[1]
    if first == 0:
        return predict_first(projections, velocity, size)
    spec = pl.BlockSpec((2, depth, HD), lambda head: (0, 0, first + head))
    return pl.pallas_call(
        predict_kernel,
        grid=(size,),
        in_specs=[spec, spec] + [ANYWHERE] * len(tokens),
        out_specs=pl.BlockSpec((depth, 2 * HD), lambda head: (0, head)),
        out_shape=jax.ShapeDtypeStruct((depth, 2 * HD * size), jnp.bfloat16),
        cost_estimate=pl.CostEstimate(
            flops=2 * depth * HD * size, bytes_accessed=16 * depth * HD * size, transcendentals=0
        ),
        name="predict",
    )(projections, velocity, *tokens)


def arrange_kernel(pos, rows, _, result, *, line, tensor_count):
    per_tensor = line // tensor_count
    slots, depth = rows.shape[3:]
    for x_at in range(2):
        for z in range(line):
            shift = lax.rem(pos[3] - z // per_tensor + tensor_count, tensor_count)
            for core in range(2):
                first = (2 * z + core) * depth
                result[x_at * slots : (x_at + 1) * slots, first : first + depth] = rows[
                    shift * per_tensor + z % per_tensor, core, lax.rem(pos[1] + x_at, 2)
                ]


def arrange(pos, rows, token, line, tensor_count):
    slots, depth = rows.shape[3:]
    return pl.pallas_call(
        functools.partial(arrange_kernel, line=line, tensor_count=tensor_count),
        in_specs=[
            pl.BlockSpec(memory_space=pltpu.SMEM),
            pl.BlockSpec(memory_space=pltpu.VMEM),
            ANYWHERE,
        ],
        out_specs=pl.BlockSpec(memory_space=pltpu.VMEM),
        out_shape=jax.ShapeDtypeStruct((2 * slots, 2 * line * depth), jnp.bfloat16),
        compiler_params=pltpu.CompilerParams(vmem_limit_bytes=VMEM_LIMIT),
        cost_estimate=pl.CostEstimate(
            flops=0, bytes_accessed=4 * rows.size, transcendentals=0
        ),
        name="arrange",
    )(pos, rows, token)


def project_kernel(rows, weights, *rest):
    mine, other = rest[-2:]
    slots = mine.shape[0]
    total = jnp.dot(rows[...], weights[...], preferred_element_type=jnp.float32)
    mine[...] = total[:slots]
    other[...] = total[slots:].astype(other.dtype)


def project(rows, weights, first, width, *tokens):
    features = weights.shape[0]
    first_block = first // HD
    slots = rows.shape[0] // 2
    result_spec = pl.BlockSpec((slots, HD), lambda at: (0, at))
    return pl.pallas_call(
        project_kernel,
        grid=(width // HD,),
        in_specs=[
            pl.BlockSpec(rows.shape, lambda at: (0, 0)),
            pl.BlockSpec((features, HD), lambda at: (0, first_block + at)),
        ]
        + [ANYWHERE] * len(tokens),
        out_specs=[result_spec, result_spec],
        out_shape=(
            jax.ShapeDtypeStruct((slots, width), jnp.float32),
            jax.ShapeDtypeStruct((slots, width), jnp.bfloat16),
        ),
        compiler_params=pltpu.CompilerParams(vmem_limit_bytes=VMEM_LIMIT),
        cost_estimate=pl.CostEstimate(
            flops=2 * 2 * slots * features * width,
            bytes_accessed=2 * features * width + rows.size * 2 + 6 * slots * width,
            transcendentals=0,
        ),
        name="project",
    )(rows, weights, *tokens)


def attend_kernel(block, live, usable, queries, grads, mine, received, *rest):
    query_grad, pair_grad, key_total, value_total = rest[-4:]
    both = (mine[...] + received[...].astype(jnp.float32)).astype(jnp.bfloat16)
    keys, values = both[:, :HD], both[:, HD:]
    scale = 1.0 / math.sqrt(HD)
    mask = usable[...]
    last_dims = (((1,), (1,)), ((), ()))
    query_count = queries.shape[0]
    for first in range(0, query_count, block):
        at = pl.ds(first, block)
        q = queries[at, :]
        position = first + lax.broadcasted_iota(jnp.int32, (block, 1), 0)
        g = grads[at, :]
        g = jnp.where(position < live[0], g, jnp.zeros_like(g))
        raw = lax.dot_general(keys, q, last_dims, preferred_element_type=jnp.float32)
        bent = jnp.tanh(raw * (scale / CAP_LIMIT))
        terms = jnp.exp(bent * CAP_LIMIT) * mask
        attention = terms * (1.0 / jnp.sum(terms, axis=0, keepdims=True))
        prob_grad = lax.dot_general(values, g, last_dims, preferred_element_type=jnp.float32)
        row_term = jnp.sum(attention * prob_grad, axis=0, keepdims=True)
        score_grad = (
            attention * (prob_grad - row_term) * ((1.0 - bent * bent) * scale)
        ).astype(jnp.bfloat16)
        rounded = attention.astype(jnp.bfloat16)
        query_grad[at, :] = lax.dot_general(
            score_grad, keys, (((0,), (0,)), ((), ())), preferred_element_type=jnp.float32
        ).astype(jnp.bfloat16)
        key_block = jnp.dot(score_grad, q, preferred_element_type=jnp.float32)
        value_block = jnp.dot(rounded, g, preferred_element_type=jnp.float32)
        if first == 0:
            key_total[...] = key_block
            value_total[...] = value_block
        else:
            key_total[...] += key_block
            value_total[...] += value_block
    pair_grad[:, :HD] = key_total[...].astype(jnp.bfloat16)
    pair_grad[:, HD:] = value_total[...].astype(jnp.bfloat16)


def attend(live, usable, queries, grads, mine, received, first_head, earlier, *tokens):
    query_count, width = queries.shape
    slots, chunk = mine.shape
    heads = chunk // (2 * HD)
    block = min(1024, query_count)
    columns = pl.BlockSpec((query_count, HD), lambda head: (0, first_head + head))
    pair = pl.BlockSpec((slots, 2 * HD), lambda head: (0, head))
    operands = [live, usable, queries, grads, mine, received]
    in_specs = [
        pl.BlockSpec(memory_space=pltpu.SMEM),
        pl.BlockSpec((slots, 1), lambda head: (0, 0)),
        columns,
        columns,
        pair,
        pair,
    ]
    aliases = {}
    if earlier is not None:
        aliases = {len(operands): 0}
        operands.append(earlier)
        in_specs.append(ANYWHERE)
    operands += tokens
    in_specs += [ANYWHERE] * len(tokens)
    return pl.pallas_call(
        functools.partial(attend_kernel, block),
        grid=(heads,),
        in_specs=in_specs,
        out_specs=[columns, pair],
        out_shape=(
            jax.ShapeDtypeStruct((query_count, width), jnp.bfloat16),
            jax.ShapeDtypeStruct((slots, chunk), jnp.bfloat16),
        ),
        scratch_shapes=[pltpu.VMEM((slots, HD), jnp.float32)] * 2,
        input_output_aliases=aliases,
        compiler_params=pltpu.CompilerParams(vmem_limit_bytes=VMEM_LIMIT),
        cost_estimate=pl.CostEstimate(
            flops=5 * query_count * slots * chunk,
            bytes_accessed=3 * query_count * chunk + 10 * slots * chunk,
            transcendentals=2 * query_count * slots * heads,
        ),
        name="attend",
    )(*operands)


def spread_kernel(pos, *refs, parts, sides, earlier):
    scratch = parts if len(sides) > 1 else 0
    result, mark = refs[len(refs) - 2 - scratch : len(refs) - scratch]
    joined = refs[len(refs) - scratch :]
    mark[...] = jnp.zeros_like(mark)
    stride = len(sides) + 1
    depth = result.shape[-1]
    slots = refs[0].shape[0]

    if scratch:

        @pl.when(pl.program_id(0) == 0)
        def _():
            for part in range(parts):
                for at in range(len(sides)):
                    joined[part][at * slots : (at + 1) * slots] = refs[stride * part + at][...]

    total = None
    for part in range(parts):
        grads = joined[part] if scratch else refs[stride * part]
        term = lax.dot_general(
            grads[...],
            refs[stride * part + stride - 1][...],
            (((1,), (1,)), ((), ())),
            preferred_element_type=jnp.float32,
        )
        total = term if total is None else total + term
    for core in range(2):
        for at in range(len(sides)):
            share = total[at * slots : (at + 1) * slots, core * depth : (core + 1) * depth]
            if earlier:
                share = share + refs[stride * parts][0, core, at].astype(jnp.float32)
            result[0, core, at] = share.astype(result.dtype)


def spread(pos, depth, units, earlier, sides, first, count, tensor_count, dtype, *tokens):
    line = units[0][2].shape[0] // (2 * depth)
    slots = units[0][0].shape[0]
    per_tensor = line // tensor_count

    def weight_at(column):
        def index(step, pos):
            block = first + step
            return (
                lax.rem(pos[3] + block // per_tensor, tensor_count) * per_tensor
                + lax.rem(block, per_tensor),
                column,
            )

        return index

    operands, in_specs, scratch, widths = [pos], [], [], 0
    for unit in units:
        width = unit[0].shape[1]
        for side in sides:
            operands.append(unit[side])
            in_specs.append(pl.BlockSpec((slots, width), lambda step, pos: (0, 0)))
        operands.append(unit[2])
        in_specs.append(pl.BlockSpec((2 * depth, width), weight_at(unit[3] // width)))
        if len(sides) > 1:
            scratch.append(pltpu.VMEM((len(sides) * slots, width), jnp.bfloat16))
        widths += width
    block = (1, 2, len(sides), slots, depth)
    if earlier is not None:
        operands.append(earlier)
        side = sides[0] if len(sides) == 1 else 0
        in_specs.append(pl.BlockSpec(block, lambda step, pos: (first + step, 0, side, 0, 0)))
    operands += tokens
    in_specs += [ANYWHERE] * len(tokens)
    return pl.pallas_call(
        functools.partial(
            spread_kernel, parts=len(units), sides=sides, earlier=earlier is not None
        ),
        grid_spec=pltpu.PrefetchScalarGridSpec(
            num_scalar_prefetch=1,
            grid=(count,),
            in_specs=in_specs,
            out_specs=[
                pl.BlockSpec(block, lambda step, pos: (step, 0, 0, 0, 0)),
                pl.BlockSpec((8, 128), lambda step, pos: (0, 0)),
            ],
            scratch_shapes=scratch,
        ),
        out_shape=(
            jax.ShapeDtypeStruct((count,) + block[1:], dtype),
            jax.ShapeDtypeStruct((8, 128), jnp.float32),
        ),
        compiler_params=pltpu.CompilerParams(vmem_limit_bytes=VMEM_LIMIT),
        cost_estimate=pl.CostEstimate(
            flops=2 * len(sides) * slots * 2 * count * depth * widths,
            bytes_accessed=4 * count * depth * widths + 8 * count * math.prod(block),
            transcendentals=0,
        ),
        name="spread",
    )(*operands)


def on_device(queries, out_grad, target_len, encoded, row_owner, projections, velocity):
    peers = lax.axis_size("dp")
    tensor_count = lax.axis_size("tensor")
    line = peers // 4
    per_tensor = line // tensor_count
    stored_rows = encoded.shape[0]
    depth = projections.shape[1]
    capacity = max(2, 2 * stored_rows // peers)
    slots = peers * capacity
    place = lax.axis_index("dp")
    tensor_at = lax.axis_index("tensor")
    pos = jnp.stack([place // 4, (place // 2) % 2, place % 2, tensor_at]).astype(jnp.int32)
    columns = [[i for i in range(peers) if (i // 2) % 2 == side] for side in range(2)]
    x_swap = [(i, i ^ 2) for i in range(peers)]

    def tensor_shift(value, shift):
        pairs = [(i, (i + shift) % tensor_count) for i in range(tensor_count)]
        return lax.ppermute(value, "tensor", pairs)

    placement = slot_table(row_owner[:, 0], capacity, peers)
    filled = jnp.sum(placement.astype(jnp.float32), axis=1).astype(jnp.bfloat16)
    outgoing = jnp.dot(placement, encoded, preferred_element_type=jnp.float32).astype(jnp.bfloat16)
    outgoing = outgoing.reshape(line, 2, 2, capacity, per_tensor, 2, 2, depth)
    outgoing = outgoing.transpose(0, 5, 2, 4, 6, 1, 3, 7).reshape(peers, -1, depth)

    incoming = lax.all_to_all(outgoing, "dp", split_axis=0, concat_axis=0, tiled=True)
    parts = []
    first, token = 0, ()
    for size in split_heads(queries.shape[1] // HD):
        block = predict(projections, velocity, first, size, *token)
        gathered = lax.all_gather(block, "dp", axis=0, tiled=True, axis_index_groups=columns)
        parts.append((first, size, gathered))
        first, token = first + size, (block, incoming)

    usable = lax.all_to_all(filled, "dp", split_axis=0, concat_axis=0, tiled=True)
    usable = (usable.astype(jnp.float32) > 0.5).astype(jnp.float32)[:, None]
    incoming = incoming.reshape(peers, per_tensor, 2, 2, capacity, depth)
    incoming = incoming.transpose(1, 2, 3, 0, 4, 5).reshape(per_tensor, 2, 2, slots, depth)
    rows = jnp.concatenate(
        [incoming] + [tensor_shift(incoming, shift) for shift in range(1, tensor_count)]
    )
    rows = arrange(pos, rows, usable, line, tensor_count)

    query_grad, token, units, early, exchanged = None, (), [], None, []
    for at, (first, size, weights) in enumerate(parts):
        final = at == len(parts) - 1
        if final:
            early, done = spread(
                pos, depth, units, None, (0, 1), 0, line, tensor_count, jnp.bfloat16
            )
            units = []
        products, column = [], 0
        for heads in split_units(size):
            width = 2 * HD * heads
            mine, other = project(rows, weights, column, width, *token)
            products.append((column, mine, lax.ppermute(other, "dp", x_swap)))
            column += width
        for column, mine, received in products:
            query_grad, pair_grad = attend(
                target_len,
                usable,
                queries,
                out_grad,
                mine,
                received,
                first + column // (2 * HD),
                query_grad,
                *((done,) if final else ()),
                *exchanged[-2:-1],
            )
            exchanged.append(lax.ppermute(pair_grad, "dp", x_swap))
            units.append((pair_grad, exchanged[-1], weights, column))
            token = (pair_grad,)

    passed, kept, marks = [], [], []
    for side in range(2):
        sent, mark = spread(
            pos, depth, units, early, (side,), per_tensor, line - per_tensor, tensor_count,
            jnp.bfloat16, *marks,
        )
        marks.append(mark)
        passed.append(
            [
                tensor_shift(sent[(shift - 1) * per_tensor : shift * per_tensor], shift)
                for shift in range(1, tensor_count)
            ]
        )
    for side in range(2):
        kept.append(
            spread(
                pos, depth, units, early, (side,), 0, per_tensor, tensor_count, jnp.float32,
                marks[side],
            )[0]
        )

    def send_home(kept, passed):
        for part in passed:
            kept = kept + part.astype(jnp.float32)
        kept = kept.astype(jnp.bfloat16).reshape(per_tensor, 2, peers, capacity, depth)
        kept = kept.transpose(2, 0, 1, 3, 4).reshape(peers, -1, depth)
        returned = lax.all_to_all(kept, "dp", split_axis=0, concat_axis=0, tiled=True)
        return returned.reshape(line, 2, 2, per_tensor, 2, capacity, depth)

    homes = placement.reshape(line, 2, 2, capacity, stored_rows)
    encoded_grad = jnp.einsum(
        "zxckr,zxcpqkd->rpxqd", homes, send_home(kept[0], passed[0]), preferred_element_type=jnp.float32
    ) + jnp.einsum(
        "zxckr,zxcpqkd->rpxqd",
        homes[:, ::-1],
        send_home(kept[1], passed[1]),
        preferred_element_type=jnp.float32,
    )
    return (query_grad, encoded_grad.astype(jnp.bfloat16).reshape(stored_rows, -1))


def solution(mesh):
    in_specs = (
        P("dp", "tensor"),
        P("dp", "tensor"),
        P("dp"),
        P("dp", "tensor"),
        P("dp", None),
        P(None, "dp", "tensor"),
        P(None, "dp", "tensor"),
    )
    out_specs = (P("dp", "tensor"), P("dp", "tensor"))
    return jax.shard_map(
        on_device, mesh=mesh, in_specs=in_specs, out_specs=out_specs, check_vma=False
    )
```

```python
import functools
import math

import jax
import jax.numpy as jnp
from jax import lax
from jax.experimental import pallas as pl
from jax.experimental.pallas import tpu as pltpu
from jax.sharding import PartitionSpec as P

HD = 256
CAP_LIMIT = 10.0
VMEM_LIMIT = 48 * 1024 * 1024
VMEM_WHOLE = 60 * 1024 * 1024


def slot_table(labels, capacity, peer_count):
    targets = (labels[:, None] == jnp.arange(peer_count, dtype=jnp.int32)[None, :]).astype(
        jnp.int32
    )
    before = jnp.cumsum(targets, axis=0) - targets
    rank_in = jnp.sum(before * targets, axis=1)
    slot_index = labels * capacity + rank_in
    placement = jnp.arange(peer_count * capacity, dtype=jnp.int32)[:, None] == slot_index[None, :]
    return placement.astype(jnp.bfloat16)


def split_heads(head_count):
    if head_count < 4:
        return [1] * head_count
    part = (3 * head_count) // 8
    return [head_count - part, part]


def split_units(size):
    return [2] * (size // 2) + [1] * (size % 2)


ANYWHERE = pl.BlockSpec(memory_space=pl.ANY)


def tie_kernel(*refs):
    pass


def tie(value, token):
    return pl.pallas_call(
        tie_kernel,
        in_specs=[ANYWHERE, ANYWHERE],
        out_specs=ANYWHERE,
        out_shape=jax.ShapeDtypeStruct(value.shape, value.dtype),
        input_output_aliases={0: 0},
        cost_estimate=pl.CostEstimate(flops=0, bytes_accessed=0, transcendentals=0),
        name="tie",
    )(value, token)


def predict_kernel(weights, velocity, *rest):
    result = rest[-1]
    for side in range(2):
        result[:, side * HD : (side + 1) * HD] = (
            weights[side].astype(jnp.float32) - velocity[side]
        ).astype(jnp.bfloat16)


def predict_first_kernel(weights, velocity, result, held_weights, held_velocity, held, sems):
    depth = weights.shape[1]
    size = held.shape[0]
    loads, stores = [], []
    for head in range(size):
        at = pl.ds(head * HD, HD)
        loads.append(
            (
                pltpu.make_async_copy(weights.at[:, :, at], held_weights.at[head], sems.at[0, head]),
                pltpu.make_async_copy(
                    velocity.at[:, :, at], held_velocity.at[head], sems.at[1, head]
                ),
            )
        )
        stores.append(
            pltpu.make_async_copy(
                held.at[head], result.at[:, pl.ds(2 * head * HD, 2 * HD)], sems.at[2, head]
            )
        )
        for load in loads[-1]:
            load.start()
    for head in range(size):
        for load in loads[head]:
            load.wait()
        for side in range(2):
            held[head, :, side * HD : (side + 1) * HD] = (
                held_weights[head, side].astype(jnp.float32) - held_velocity[head, side]
            ).astype(jnp.bfloat16)
        stores[head].start()
    for store in stores:
        store.wait()


def predict_first(projections, velocity, size):
    depth = projections.shape[1]
    return pl.pallas_call(
        predict_first_kernel,
        in_specs=[ANYWHERE, ANYWHERE],
        out_specs=ANYWHERE,
        out_shape=jax.ShapeDtypeStruct((depth, 2 * HD * size), jnp.bfloat16),
        scratch_shapes=[
            pltpu.VMEM((size, 2, depth, HD), jnp.bfloat16),
            pltpu.VMEM((size, 2, depth, HD), jnp.float32),
            pltpu.VMEM((size, depth, 2 * HD), jnp.bfloat16),
            pltpu.SemaphoreType.DMA((3, size)),
        ],
        compiler_params=pltpu.CompilerParams(vmem_limit_bytes=VMEM_WHOLE),
        cost_estimate=pl.CostEstimate(
            flops=2 * depth * HD * size, bytes_accessed=16 * depth * HD * size, transcendentals=0
        ),
        name="predict_first",
    )(projections, velocity)


def predict(projections, velocity, first, size, *tokens):
    depth = projections.shape[1]
    if first == 0:
        return predict_first(projections, velocity, size)
    spec = pl.BlockSpec((2, depth, HD), lambda head: (0, 0, first + head))
    return pl.pallas_call(
        predict_kernel,
        grid=(size,),
        in_specs=[spec, spec] + [ANYWHERE] * len(tokens),
        out_specs=pl.BlockSpec((depth, 2 * HD), lambda head: (0, head)),
        out_shape=jax.ShapeDtypeStruct((depth, 2 * HD * size), jnp.bfloat16),
        cost_estimate=pl.CostEstimate(
            flops=2 * depth * HD * size, bytes_accessed=16 * depth * HD * size, transcendentals=0
        ),
        name="predict",
    )(projections, velocity, *tokens)


def arrange_kernel(pos, rows, _, result, *, line, tensor_count):
    per_tensor = line // tensor_count
    slots, depth = rows.shape[3:]
    for x_at in range(2):
        for z in range(line):
            shift = lax.rem(pos[3] - z // per_tensor + tensor_count, tensor_count)
            for core in range(2):
                first = (2 * z + core) * depth
                result[x_at * slots : (x_at + 1) * slots, first : first + depth] = rows[
                    shift * per_tensor + z % per_tensor, core, lax.rem(pos[1] + x_at, 2)
                ]


def arrange(pos, rows, token, line, tensor_count):
    slots, depth = rows.shape[3:]
    return pl.pallas_call(
        functools.partial(arrange_kernel, line=line, tensor_count=tensor_count),
        in_specs=[
            pl.BlockSpec(memory_space=pltpu.SMEM),
            pl.BlockSpec(memory_space=pltpu.VMEM),
            ANYWHERE,
        ],
        out_specs=pl.BlockSpec(memory_space=pltpu.VMEM),
        out_shape=jax.ShapeDtypeStruct((2 * slots, 2 * line * depth), jnp.bfloat16),
        compiler_params=pltpu.CompilerParams(vmem_limit_bytes=VMEM_LIMIT),
        cost_estimate=pl.CostEstimate(
            flops=0, bytes_accessed=4 * rows.size, transcendentals=0
        ),
        name="arrange",
    )(pos, rows, token)


def project_kernel(rows, weights, *rest):
    mine, other = rest[-2:]
    slots = mine.shape[0]
    total = jnp.dot(rows[...], weights[...], preferred_element_type=jnp.float32)
    mine[...] = total[:slots]
    other[...] = total[slots:].astype(other.dtype)


def project(rows, weights, first, width, *tokens):
    features = weights.shape[0]
    first_block = first // HD
    slots = rows.shape[0] // 2
    result_spec = pl.BlockSpec((slots, HD), lambda at: (0, at))
    return pl.pallas_call(
        project_kernel,
        grid=(width // HD,),
        in_specs=[
            pl.BlockSpec(rows.shape, lambda at: (0, 0)),
            pl.BlockSpec((features, HD), lambda at: (0, first_block + at)),
        ]
        + [ANYWHERE] * len(tokens),
        out_specs=[result_spec, result_spec],
        out_shape=(
            jax.ShapeDtypeStruct((slots, width), jnp.float32),
            jax.ShapeDtypeStruct((slots, width), jnp.bfloat16),
        ),
        compiler_params=pltpu.CompilerParams(vmem_limit_bytes=VMEM_LIMIT),
        cost_estimate=pl.CostEstimate(
            flops=2 * 2 * slots * features * width,
            bytes_accessed=2 * features * width + rows.size * 2 + 6 * slots * width,
            transcendentals=0,
        ),
        name="project",
    )(rows, weights, *tokens)


def attend_kernel(block, live, usable, queries, grads, mine, received, *rest):
    query_grad, pair_grad, key_total, value_total = rest[-4:]
    both = (mine[...] + received[...].astype(jnp.float32)).astype(jnp.bfloat16)
    keys, values = both[:, :HD], both[:, HD:]
    scale = 1.0 / math.sqrt(HD)
    mask = usable[...]
    last_dims = (((1,), (1,)), ((), ()))
    query_count = queries.shape[0]
    for first in range(0, query_count, block):
        at = pl.ds(first, block)
        q = queries[at, :]
        position = first + lax.broadcasted_iota(jnp.int32, (block, 1), 0)
        g = grads[at, :]
        g = jnp.where(position < live[0], g, jnp.zeros_like(g))
        raw = lax.dot_general(keys, q, last_dims, preferred_element_type=jnp.float32)
        bent = jnp.tanh(raw * (scale / CAP_LIMIT))
        terms = jnp.exp(bent * CAP_LIMIT) * mask
        attention = terms * (1.0 / jnp.sum(terms, axis=0, keepdims=True))
        prob_grad = lax.dot_general(values, g, last_dims, preferred_element_type=jnp.float32)
        row_term = jnp.sum(attention * prob_grad, axis=0, keepdims=True)
        score_grad = (
            attention * (prob_grad - row_term) * ((1.0 - bent * bent) * scale)
        ).astype(jnp.bfloat16)
        rounded = attention.astype(jnp.bfloat16)
        query_grad[at, :] = lax.dot_general(
            score_grad, keys, (((0,), (0,)), ((), ())), preferred_element_type=jnp.float32
        ).astype(jnp.bfloat16)
        key_block = jnp.dot(score_grad, q, preferred_element_type=jnp.float32)
        value_block = jnp.dot(rounded, g, preferred_element_type=jnp.float32)
        if first == 0:
            key_total[...] = key_block
            value_total[...] = value_block
        else:
            key_total[...] += key_block
            value_total[...] += value_block
    pair_grad[:, :HD] = key_total[...].astype(jnp.bfloat16)
    pair_grad[:, HD:] = value_total[...].astype(jnp.bfloat16)


def attend(live, usable, queries, grads, mine, received, first_head, earlier, *tokens):
    query_count, width = queries.shape
    slots, chunk = mine.shape
    heads = chunk // (2 * HD)
    block = min(1024, query_count)
    columns = pl.BlockSpec((query_count, HD), lambda head: (0, first_head + head))
    pair = pl.BlockSpec((slots, 2 * HD), lambda head: (0, head))
    operands = [live, usable, queries, grads, mine, received]
    in_specs = [
        pl.BlockSpec(memory_space=pltpu.SMEM),
        pl.BlockSpec((slots, 1), lambda head: (0, 0)),
        columns,
        columns,
        pair,
        pair,
    ]
    aliases = {}
    if earlier is not None:
        aliases = {len(operands): 0}
        operands.append(earlier)
        in_specs.append(ANYWHERE)
    operands += tokens
    in_specs += [ANYWHERE] * len(tokens)
    return pl.pallas_call(
        functools.partial(attend_kernel, block),
        grid=(heads,),
        in_specs=in_specs,
        out_specs=[columns, pair],
        out_shape=(
            jax.ShapeDtypeStruct((query_count, width), jnp.bfloat16),
            jax.ShapeDtypeStruct((slots, chunk), jnp.bfloat16),
        ),
        scratch_shapes=[pltpu.VMEM((slots, HD), jnp.float32)] * 2,
        input_output_aliases=aliases,
        compiler_params=pltpu.CompilerParams(vmem_limit_bytes=VMEM_LIMIT),
        cost_estimate=pl.CostEstimate(
            flops=5 * query_count * slots * chunk,
            bytes_accessed=3 * query_count * chunk + 10 * slots * chunk,
            transcendentals=2 * query_count * slots * heads,
        ),
        name="attend",
    )(*operands)


def spread_kernel(pos, *refs, parts, sides, earlier):
    scratch = parts if len(sides) > 1 else 0
    result, mark = refs[len(refs) - 2 - scratch : len(refs) - scratch]
    joined = refs[len(refs) - scratch :]
    mark[...] = jnp.zeros_like(mark)
    stride = len(sides) + 1
    depth = result.shape[-1]
    slots = refs[0].shape[0]

    if scratch:

        @pl.when(pl.program_id(0) == 0)
        def _():
            for part in range(parts):
                for at in range(len(sides)):
                    joined[part][at * slots : (at + 1) * slots] = refs[stride * part + at][...]

    total = None
    for part in range(parts):
        grads = joined[part] if scratch else refs[stride * part]
        term = lax.dot_general(
            grads[...],
            refs[stride * part + stride - 1][...],
            (((1,), (1,)), ((), ())),
            preferred_element_type=jnp.float32,
        )
        total = term if total is None else total + term
    for core in range(2):
        for at in range(len(sides)):
            share = total[at * slots : (at + 1) * slots, core * depth : (core + 1) * depth]
            if earlier:
                share = share + refs[stride * parts][0, core, at].astype(jnp.float32)
            result[0, core, at] = share.astype(result.dtype)


def spread(pos, depth, units, earlier, sides, first, count, tensor_count, dtype, *tokens):
    line = units[0][2].shape[0] // (2 * depth)
    slots = units[0][0].shape[0]
    per_tensor = line // tensor_count

    def weight_at(column):
        def index(step, pos):
            block = first + step
            return (
                lax.rem(pos[3] + block // per_tensor, tensor_count) * per_tensor
                + lax.rem(block, per_tensor),
                column,
            )

        return index

    operands, in_specs, scratch, widths = [pos], [], [], 0
    for unit in units:
        width = unit[0].shape[1]
        for side in sides:
            operands.append(unit[side])
            in_specs.append(pl.BlockSpec((slots, width), lambda step, pos: (0, 0)))
        operands.append(unit[2])
        in_specs.append(pl.BlockSpec((2 * depth, width), weight_at(unit[3] // width)))
        if len(sides) > 1:
            scratch.append(pltpu.VMEM((len(sides) * slots, width), jnp.bfloat16))
        widths += width
    block = (1, 2, len(sides), slots, depth)
    if earlier is not None:
        operands.append(earlier)
        side = sides[0] if len(sides) == 1 else 0
        in_specs.append(pl.BlockSpec(block, lambda step, pos: (first + step, 0, side, 0, 0)))
    operands += tokens
    in_specs += [ANYWHERE] * len(tokens)
    return pl.pallas_call(
        functools.partial(
            spread_kernel, parts=len(units), sides=sides, earlier=earlier is not None
        ),
        grid_spec=pltpu.PrefetchScalarGridSpec(
            num_scalar_prefetch=1,
            grid=(count,),
            in_specs=in_specs,
            out_specs=[
                pl.BlockSpec(block, lambda step, pos: (step, 0, 0, 0, 0)),
                pl.BlockSpec((8, 128), lambda step, pos: (0, 0)),
            ],
            scratch_shapes=scratch,
        ),
        out_shape=(
            jax.ShapeDtypeStruct((count,) + block[1:], dtype),
            jax.ShapeDtypeStruct((8, 128), jnp.float32),
        ),
        compiler_params=pltpu.CompilerParams(vmem_limit_bytes=VMEM_LIMIT),
        cost_estimate=pl.CostEstimate(
            flops=2 * len(sides) * slots * 2 * count * depth * widths,
            bytes_accessed=4 * count * depth * widths + 8 * count * math.prod(block),
            transcendentals=0,
        ),
        name="spread",
    )(*operands)


def on_device(queries, out_grad, target_len, encoded, row_owner, projections, velocity):
    peers = lax.axis_size("dp")
    tensor_count = lax.axis_size("tensor")
    line = peers // 4
    per_tensor = line // tensor_count
    stored_rows = encoded.shape[0]
    depth = projections.shape[1]
    capacity = max(2, 2 * stored_rows // peers)
    slots = peers * capacity
    place = lax.axis_index("dp")
    tensor_at = lax.axis_index("tensor")
    pos = jnp.stack([place // 4, (place // 2) % 2, place % 2, tensor_at]).astype(jnp.int32)
    columns = [[i for i in range(peers) if (i // 2) % 2 == side] for side in range(2)]
    x_swap = [(i, i ^ 2) for i in range(peers)]

    def tensor_shift(value, shift):
        pairs = [(i, (i + shift) % tensor_count) for i in range(tensor_count)]
        return lax.ppermute(value, "tensor", pairs)

    placement = slot_table(row_owner[:, 0], capacity, peers)
    filled = jnp.sum(placement.astype(jnp.float32), axis=1).astype(jnp.bfloat16)
    outgoing = jnp.dot(placement, encoded, preferred_element_type=jnp.float32).astype(jnp.bfloat16)
    outgoing = outgoing.reshape(line, 2, 2, capacity, per_tensor, 2, 2, depth)
    outgoing = outgoing.transpose(0, 5, 2, 4, 6, 1, 3, 7).reshape(peers, -1, depth)

    incoming = lax.all_to_all(outgoing, "dp", split_axis=0, concat_axis=0, tiled=True)
    parts = []
    first, token = 0, ()
    for size in split_heads(queries.shape[1] // HD):
        block = predict(projections, velocity, first, size, *token)
        gathered = lax.all_gather(block, "dp", axis=0, tiled=True, axis_index_groups=columns)
        parts.append((first, size, gathered))
        first, token = first + size, (block, incoming)

    usable = lax.all_to_all(filled, "dp", split_axis=0, concat_axis=0, tiled=True)
    usable = (usable.astype(jnp.float32) > 0.5).astype(jnp.float32)[:, None]
    incoming = incoming.reshape(peers, per_tensor, 2, 2, capacity, depth)
    incoming = incoming.transpose(1, 2, 3, 0, 4, 5).reshape(per_tensor, 2, 2, slots, depth)
    rows = jnp.concatenate(
        [incoming] + [tensor_shift(incoming, shift) for shift in range(1, tensor_count)]
    )
    rows = arrange(pos, rows, usable, line, tensor_count)

    query_grad, token, units, early, exchanged = None, (), [], None, []
    for at, (first, size, weights) in enumerate(parts):
        final = at == len(parts) - 1
        if final:
            early, done = spread(
                pos, depth, units, None, (0, 1), 0, line, tensor_count, jnp.bfloat16
            )
            units = []
        products, column = [], 0
        for heads in split_units(size):
            width = 2 * HD * heads
            mine, other = project(rows, weights, column, width, *token)
            products.append((column, mine, lax.ppermute(other, "dp", x_swap)))
            column += width
        for column, mine, received in products:
            query_grad, pair_grad = attend(
                target_len,
                usable,
                queries,
                out_grad,
                mine,
                received,
                first + column // (2 * HD),
                query_grad,
                *((done,) if final else ()),
            )
            exchanged.append(lax.ppermute(pair_grad, "dp", x_swap))
            units.append((pair_grad, exchanged[-1], weights, column))
            token = (pair_grad,)

    passed, kept, marks = [], [], []
    for side in range(2):
        sent, mark = spread(
            pos, depth, units, early, (side,), per_tensor, line - per_tensor, tensor_count,
            jnp.bfloat16, *marks,
        )
        marks.append(mark)
        passed.append(
            [
                tensor_shift(sent[(shift - 1) * per_tensor : shift * per_tensor], shift)
                for shift in range(1, tensor_count)
            ]
        )
    for side in range(2):
        kept.append(
            spread(
                pos, depth, units, early, (side,), 0, per_tensor, tensor_count, jnp.float32,
                marks[side],
            )[0]
        )

    def send_home(kept, passed):
        for part in passed:
            kept = kept + part.astype(jnp.float32)
        kept = kept.astype(jnp.bfloat16).reshape(per_tensor, 2, peers, capacity, depth)
        kept = kept.transpose(2, 0, 1, 3, 4).reshape(peers, -1, depth)
        returned = lax.all_to_all(kept, "dp", split_axis=0, concat_axis=0, tiled=True)
        return returned.reshape(line, 2, 2, per_tensor, 2, capacity, depth)

    homes = placement.reshape(line, 2, 2, capacity, stored_rows)
    encoded_grad = jnp.einsum(
        "zxckr,zxcpqkd->rpxqd", homes, send_home(kept[0], passed[0]), preferred_element_type=jnp.float32
    ) + jnp.einsum(
        "zxckr,zxcpqkd->rpxqd",
        homes[:, ::-1],
        send_home(kept[1], passed[1]),
        preferred_element_type=jnp.float32,
    )
    return (query_grad, encoded_grad.astype(jnp.bfloat16).reshape(stored_rows, -1))


def solution(mesh):
    in_specs = (
        P("dp", "tensor"),
        P("dp", "tensor"),
        P("dp"),
        P("dp", "tensor"),
        P("dp", None),
        P(None, "dp", "tensor"),
        P(None, "dp", "tensor"),
    )
    out_specs = (P("dp", "tensor"), P("dp", "tensor"))
    return jax.shard_map(
        on_device, mesh=mesh, in_specs=in_specs, out_specs=out_specs, check_vma=False
    )
```

```python
import functools
import math

import jax
import jax.numpy as jnp
from jax import lax
from jax.experimental import pallas as pl
from jax.experimental.pallas import tpu as pltpu
from jax.sharding import PartitionSpec as P

HD = 256
CAP_LIMIT = 10.0
VMEM_LIMIT = 48 * 1024 * 1024
VMEM_WHOLE = 60 * 1024 * 1024


def slot_table(labels, capacity, peer_count):
    targets = (labels[:, None] == jnp.arange(peer_count, dtype=jnp.int32)[None, :]).astype(
        jnp.int32
    )
    before = jnp.cumsum(targets, axis=0) - targets
    rank_in = jnp.sum(before * targets, axis=1)
    slot_index = labels * capacity + rank_in
    placement = jnp.arange(peer_count * capacity, dtype=jnp.int32)[:, None] == slot_index[None, :]
    return placement.astype(jnp.bfloat16)


def split_heads(head_count):
    if head_count < 4:
        return [1] * head_count
    part = (3 * head_count) // 8
    return [head_count - part, part]


def split_units(size):
    return [2] * (size // 2) + [1] * (size % 2)


ANYWHERE = pl.BlockSpec(memory_space=pl.ANY)


def tie_kernel(*refs):
    pass


def tie(value, token):
    return pl.pallas_call(
        tie_kernel,
        in_specs=[ANYWHERE, ANYWHERE],
        out_specs=ANYWHERE,
        out_shape=jax.ShapeDtypeStruct(value.shape, value.dtype),
        input_output_aliases={0: 0},
        cost_estimate=pl.CostEstimate(flops=0, bytes_accessed=0, transcendentals=0),
        name="tie",
    )(value, token)


def predict_kernel(weights, velocity, *rest):
    result = rest[-1]
    for side in range(2):
        result[:, side * HD : (side + 1) * HD] = (
            weights[side].astype(jnp.float32) - velocity[side]
        ).astype(jnp.bfloat16)


def predict_first_kernel(weights, velocity, result, held_weights, held_velocity, held, sems):
    depth = weights.shape[1]
    size = held.shape[0]
    loads, stores = [], []
    for head in range(size):
        at = pl.ds(head * HD, HD)
        loads.append(
            (
                pltpu.make_async_copy(weights.at[:, :, at], held_weights.at[head], sems.at[0, head]),
                pltpu.make_async_copy(
                    velocity.at[:, :, at], held_velocity.at[head], sems.at[1, head]
                ),
            )
        )
        stores.append(
            pltpu.make_async_copy(
                held.at[head], result.at[:, pl.ds(2 * head * HD, 2 * HD)], sems.at[2, head]
            )
        )
        for load in loads[-1]:
            load.start()
    for head in range(size):
        for load in loads[head]:
            load.wait()
        for side in range(2):
            held[head, :, side * HD : (side + 1) * HD] = (
                held_weights[head, side].astype(jnp.float32) - held_velocity[head, side]
            ).astype(jnp.bfloat16)
        stores[head].start()
    for store in stores:
        store.wait()


def predict_first(projections, velocity, size):
    depth = projections.shape[1]
    return pl.pallas_call(
        predict_first_kernel,
        in_specs=[ANYWHERE, ANYWHERE],
        out_specs=ANYWHERE,
        out_shape=jax.ShapeDtypeStruct((depth, 2 * HD * size), jnp.bfloat16),
        scratch_shapes=[
            pltpu.VMEM((size, 2, depth, HD), jnp.bfloat16),
            pltpu.VMEM((size, 2, depth, HD), jnp.float32),
            pltpu.VMEM((size, depth, 2 * HD), jnp.bfloat16),
            pltpu.SemaphoreType.DMA((3, size)),
        ],
        compiler_params=pltpu.CompilerParams(vmem_limit_bytes=VMEM_WHOLE),
        cost_estimate=pl.CostEstimate(
            flops=2 * depth * HD * size, bytes_accessed=16 * depth * HD * size, transcendentals=0
        ),
        name="predict_first",
    )(projections, velocity)


def predict(projections, velocity, first, size, *tokens):
    depth = projections.shape[1]
    if first == 0:
        return predict_first(projections, velocity, size)
    spec = pl.BlockSpec((2, depth, HD), lambda head: (0, 0, first + head))
    return pl.pallas_call(
        predict_kernel,
        grid=(size,),
        in_specs=[spec, spec] + [ANYWHERE] * len(tokens),
        out_specs=pl.BlockSpec((depth, 2 * HD), lambda head: (0, head)),
        out_shape=jax.ShapeDtypeStruct((depth, 2 * HD * size), jnp.bfloat16),
        cost_estimate=pl.CostEstimate(
            flops=2 * depth * HD * size, bytes_accessed=16 * depth * HD * size, transcendentals=0
        ),
        name="predict",
    )(projections, velocity, *tokens)


def arrange_kernel(pos, rows, _, result, *, line, tensor_count):
    per_tensor = line // tensor_count
    slots, depth = rows.shape[3:]
    for x_at in range(2):
        for z in range(line):
            shift = lax.rem(pos[3] - z // per_tensor + tensor_count, tensor_count)
            for core in range(2):
                first = (2 * z + core) * depth
                result[x_at * slots : (x_at + 1) * slots, first : first + depth] = rows[
                    shift * per_tensor + z % per_tensor, core, lax.rem(pos[1] + x_at, 2)
                ]


def arrange(pos, rows, token, line, tensor_count):
    slots, depth = rows.shape[3:]
    return pl.pallas_call(
        functools.partial(arrange_kernel, line=line, tensor_count=tensor_count),
        in_specs=[
            pl.BlockSpec(memory_space=pltpu.SMEM),
            pl.BlockSpec(memory_space=pltpu.VMEM),
            ANYWHERE,
        ],
        out_specs=pl.BlockSpec(memory_space=pltpu.VMEM),
        out_shape=jax.ShapeDtypeStruct((2 * slots, 2 * line * depth), jnp.bfloat16),
        compiler_params=pltpu.CompilerParams(vmem_limit_bytes=VMEM_LIMIT),
        cost_estimate=pl.CostEstimate(
            flops=0, bytes_accessed=4 * rows.size, transcendentals=0
        ),
        name="arrange",
    )(pos, rows, token)


def project_kernel(rows, weights, *rest):
    mine, other = rest[-2:]
    slots = mine.shape[0]
    total = jnp.dot(rows[...], weights[...], preferred_element_type=jnp.float32)
    mine[...] = total[:slots]
    other[...] = total[slots:].astype(other.dtype)


def project(rows, weights, first, width, *tokens):
    features = weights.shape[0]
    first_block = first // HD
    slots = rows.shape[0] // 2
    result_spec = pl.BlockSpec((slots, HD), lambda at: (0, at))
    return pl.pallas_call(
        project_kernel,
        grid=(width // HD,),
        in_specs=[
            pl.BlockSpec(rows.shape, lambda at: (0, 0)),
            pl.BlockSpec((features, HD), lambda at: (0, first_block + at)),
        ]
        + [ANYWHERE] * len(tokens),
        out_specs=[result_spec, result_spec],
        out_shape=(
            jax.ShapeDtypeStruct((slots, width), jnp.float32),
            jax.ShapeDtypeStruct((slots, width), jnp.bfloat16),
        ),
        compiler_params=pltpu.CompilerParams(vmem_limit_bytes=VMEM_LIMIT),
        cost_estimate=pl.CostEstimate(
            flops=2 * 2 * slots * features * width,
            bytes_accessed=2 * features * width + rows.size * 2 + 6 * slots * width,
            transcendentals=0,
        ),
        name="project",
    )(rows, weights, *tokens)


def attend_kernel(block, live, usable, queries, grads, mine, received, *rest):
    query_grad, pair_grad, key_total, value_total = rest[-4:]
    both = (mine[...] + received[...].astype(jnp.float32)).astype(jnp.bfloat16)
    keys, values = both[:, :HD], both[:, HD:]
    scale = 1.0 / math.sqrt(HD)
    mask = usable[...]
    last_dims = (((1,), (1,)), ((), ()))
    query_count = queries.shape[0]
    for first in range(0, query_count, block):
        at = pl.ds(first, block)
        q = queries[at, :]
        position = first + lax.broadcasted_iota(jnp.int32, (block, 1), 0)
        g = grads[at, :]
        g = jnp.where(position < live[0], g, jnp.zeros_like(g))
        raw = lax.dot_general(keys, q, last_dims, preferred_element_type=jnp.float32)
        bent = jnp.tanh(raw * (scale / CAP_LIMIT))
        terms = jnp.exp(bent * CAP_LIMIT) * mask
        attention = terms * (1.0 / jnp.sum(terms, axis=0, keepdims=True))
        prob_grad = lax.dot_general(values, g, last_dims, preferred_element_type=jnp.float32)
        row_term = jnp.sum(attention * prob_grad, axis=0, keepdims=True)
        score_grad = (
            attention * (prob_grad - row_term) * ((1.0 - bent * bent) * scale)
        ).astype(jnp.bfloat16)
        rounded = attention.astype(jnp.bfloat16)
        query_grad[at, :] = lax.dot_general(
            score_grad, keys, (((0,), (0,)), ((), ())), preferred_element_type=jnp.float32
        ).astype(jnp.bfloat16)
        key_block = jnp.dot(score_grad, q, preferred_element_type=jnp.float32)
        value_block = jnp.dot(rounded, g, preferred_element_type=jnp.float32)
        if first == 0:
            key_total[...] = key_block
            value_total[...] = value_block
        else:
            key_total[...] += key_block
            value_total[...] += value_block
    pair_grad[:, :HD] = key_total[...].astype(jnp.bfloat16)
    pair_grad[:, HD:] = value_total[...].astype(jnp.bfloat16)


def attend(live, usable, queries, grads, mine, received, first_head, earlier, *tokens):
    query_count, width = queries.shape
    slots, chunk = mine.shape
    heads = chunk // (2 * HD)
    block = min(1024, query_count)
    columns = pl.BlockSpec((query_count, HD), lambda head: (0, first_head + head))
    pair = pl.BlockSpec((slots, 2 * HD), lambda head: (0, head))
    operands = [live, usable, queries, grads, mine, received]
    in_specs = [
        pl.BlockSpec(memory_space=pltpu.SMEM),
        pl.BlockSpec((slots, 1), lambda head: (0, 0)),
        columns,
        columns,
        pair,
        pair,
    ]
    aliases = {}
    if earlier is not None:
        aliases = {len(operands): 0}
        operands.append(earlier)
        in_specs.append(ANYWHERE)
    operands += tokens
    in_specs += [ANYWHERE] * len(tokens)
    return pl.pallas_call(
        functools.partial(attend_kernel, block),
        grid=(heads,),
        in_specs=in_specs,
        out_specs=[columns, pair],
        out_shape=(
            jax.ShapeDtypeStruct((query_count, width), jnp.bfloat16),
            jax.ShapeDtypeStruct((slots, chunk), jnp.bfloat16),
        ),
        scratch_shapes=[pltpu.VMEM((slots, HD), jnp.float32)] * 2,
        input_output_aliases=aliases,
        compiler_params=pltpu.CompilerParams(vmem_limit_bytes=VMEM_LIMIT),
        cost_estimate=pl.CostEstimate(
            flops=5 * query_count * slots * chunk,
            bytes_accessed=3 * query_count * chunk + 10 * slots * chunk,
            transcendentals=2 * query_count * slots * heads,
        ),
        name="attend",
    )(*operands)


def spread_kernel(pos, *refs, parts, sides, earlier):
    scratch = parts if len(sides) > 1 else 0
    result, mark = refs[len(refs) - 2 - scratch : len(refs) - scratch]
    joined = refs[len(refs) - scratch :]
    mark[...] = jnp.zeros_like(mark)
    stride = len(sides) + 1
    depth = result.shape[-1]
    slots = refs[0].shape[0]

    if scratch:

        @pl.when(pl.program_id(0) == 0)
        def _():
            for part in range(parts):
                for at in range(len(sides)):
                    joined[part][at * slots : (at + 1) * slots] = refs[stride * part + at][...]

    total = None
    for part in range(parts):
        grads = joined[part] if scratch else refs[stride * part]
        term = lax.dot_general(
            grads[...],
            refs[stride * part + stride - 1][...],
            (((1,), (1,)), ((), ())),
            preferred_element_type=jnp.float32,
        )
        total = term if total is None else total + term
    for core in range(2):
        for at in range(len(sides)):
            share = total[at * slots : (at + 1) * slots, core * depth : (core + 1) * depth]
            if earlier:
                share = share + refs[stride * parts][0, core, at].astype(jnp.float32)
            result[0, core, at] = share.astype(result.dtype)


def spread(pos, depth, units, earlier, sides, first, count, tensor_count, dtype, *tokens):
    line = units[0][2].shape[0] // (2 * depth)
    slots = units[0][0].shape[0]
    per_tensor = line // tensor_count

    def weight_at(column):
        def index(step, pos):
            block = first + step
            return (
                lax.rem(pos[3] + block // per_tensor, tensor_count) * per_tensor
                + lax.rem(block, per_tensor),
                column,
            )

        return index

    operands, in_specs, scratch, widths = [pos], [], [], 0
    for unit in units:
        width = unit[0].shape[1]
        for side in sides:
            operands.append(unit[side])
            in_specs.append(pl.BlockSpec((slots, width), lambda step, pos: (0, 0)))
        operands.append(unit[2])
        in_specs.append(pl.BlockSpec((2 * depth, width), weight_at(unit[3] // width)))
        if len(sides) > 1:
            scratch.append(pltpu.VMEM((len(sides) * slots, width), jnp.bfloat16))
        widths += width
    block = (1, 2, len(sides), slots, depth)
    if earlier is not None:
        operands.append(earlier)
        side = sides[0] if len(sides) == 1 else 0
        in_specs.append(pl.BlockSpec(block, lambda step, pos: (first + step, 0, side, 0, 0)))
    operands += tokens
    in_specs += [ANYWHERE] * len(tokens)
    return pl.pallas_call(
        functools.partial(
            spread_kernel, parts=len(units), sides=sides, earlier=earlier is not None
        ),
        grid_spec=pltpu.PrefetchScalarGridSpec(
            num_scalar_prefetch=1,
            grid=(count,),
            in_specs=in_specs,
            out_specs=[
                pl.BlockSpec(block, lambda step, pos: (step, 0, 0, 0, 0)),
                pl.BlockSpec((8, 128), lambda step, pos: (0, 0)),
            ],
            scratch_shapes=scratch,
        ),
        out_shape=(
            jax.ShapeDtypeStruct((count,) + block[1:], dtype),
            jax.ShapeDtypeStruct((8, 128), jnp.float32),
        ),
        compiler_params=pltpu.CompilerParams(vmem_limit_bytes=VMEM_LIMIT),
        cost_estimate=pl.CostEstimate(
            flops=2 * len(sides) * slots * 2 * count * depth * widths,
            bytes_accessed=4 * count * depth * widths + 8 * count * math.prod(block),
            transcendentals=0,
        ),
        name="spread",
    )(*operands)


def on_device(queries, out_grad, target_len, encoded, row_owner, projections, velocity):
    peers = lax.axis_size("dp")
    tensor_count = lax.axis_size("tensor")
    line = peers // 4
    per_tensor = line // tensor_count
    stored_rows = encoded.shape[0]
    depth = projections.shape[1]
    capacity = max(2, 2 * stored_rows // peers)
    slots = peers * capacity
    place = lax.axis_index("dp")
    tensor_at = lax.axis_index("tensor")
    pos = jnp.stack([place // 4, (place // 2) % 2, place % 2, tensor_at]).astype(jnp.int32)
    columns = [[i for i in range(peers) if (i // 2) % 2 == side] for side in range(2)]
    x_swap = [(i, i ^ 2) for i in range(peers)]

    def tensor_shift(value, shift):
        pairs = [(i, (i + shift) % tensor_count) for i in range(tensor_count)]
        return lax.ppermute(value, "tensor", pairs)

    placement = slot_table(row_owner[:, 0], capacity, peers)
    filled = jnp.sum(placement.astype(jnp.float32), axis=1).astype(jnp.bfloat16)
    outgoing = jnp.dot(placement, encoded, preferred_element_type=jnp.float32).astype(jnp.bfloat16)
    outgoing = outgoing.reshape(line, 2, 2, capacity, per_tensor, 2, 2, depth)
    outgoing = outgoing.transpose(0, 5, 2, 4, 6, 1, 3, 7).reshape(peers, -1, depth)

    incoming = lax.all_to_all(outgoing, "dp", split_axis=0, concat_axis=0, tiled=True)
    parts = []
    first, token = 0, ()
    for size in split_heads(queries.shape[1] // HD):
        block = predict(projections, velocity, first, size, *token)
        gathered = lax.all_gather(block, "dp", axis=0, tiled=True, axis_index_groups=columns)
        parts.append((first, size, gathered))
        first, token = first + size, (block, incoming)

    usable = lax.all_to_all(filled, "dp", split_axis=0, concat_axis=0, tiled=True)
    usable = (usable.astype(jnp.float32) > 0.5).astype(jnp.float32)[:, None]
    incoming = incoming.reshape(peers, per_tensor, 2, 2, capacity, depth)
    incoming = incoming.transpose(1, 2, 3, 0, 4, 5).reshape(per_tensor, 2, 2, slots, depth)
    rows = jnp.concatenate(
        [incoming] + [tensor_shift(incoming, shift) for shift in range(1, tensor_count)]
    )
    rows = arrange(pos, rows, usable, line, tensor_count)

    query_grad, token, units, early, exchanged = None, (), [], None, []
    for at, (first, size, weights) in enumerate(parts):
        final = at == len(parts) - 1
        if final:
            early, done = spread(
                pos, depth, units, None, (0, 1), 0, line, tensor_count, jnp.bfloat16
            )
            units = []
        spans, column = [], 0
        for heads in split_units(size):
            spans.append((column, 2 * HD * heads))
            column += 2 * HD * heads
        products = []
        for column, width in reversed(spans) if final else spans:
            mine, other = project(rows, weights, column, width, *token)
            products.append((column, mine, lax.ppermute(other, "dp", x_swap)))
        for column, mine, received in products:
            query_grad, pair_grad = attend(
                target_len,
                usable,
                queries,
                out_grad,
                mine,
                received,
                first + column // (2 * HD),
                query_grad,
                *((done,) if final else ()),
                *exchanged[-2:-1],
            )
            exchanged.append(lax.ppermute(pair_grad, "dp", x_swap))
            units.append((pair_grad, exchanged[-1], weights, column))
            token = (pair_grad,)

    passed, kept, marks = [], [], []
    for side in range(2):
        sent, mark = spread(
            pos, depth, units, early, (side,), per_tensor, line - per_tensor, tensor_count,
            jnp.bfloat16, *marks,
        )
        marks.append(mark)
        passed.append(
            [
                tensor_shift(sent[(shift - 1) * per_tensor : shift * per_tensor], shift)
                for shift in range(1, tensor_count)
            ]
        )
    for side in range(2):
        kept.append(
            spread(
                pos, depth, units, early, (side,), 0, per_tensor, tensor_count, jnp.float32,
                marks[side],
            )[0]
        )

    def send_home(kept, passed):
        for part in passed:
            kept = kept + part.astype(jnp.float32)
        kept = kept.astype(jnp.bfloat16).reshape(per_tensor, 2, peers, capacity, depth)
        kept = kept.transpose(2, 0, 1, 3, 4).reshape(peers, -1, depth)
        returned = lax.all_to_all(kept, "dp", split_axis=0, concat_axis=0, tiled=True)
        return returned.reshape(line, 2, 2, per_tensor, 2, capacity, depth)

    homes = placement.reshape(line, 2, 2, capacity, stored_rows)
    encoded_grad = jnp.einsum(
        "zxckr,zxcpqkd->rpxqd", homes, send_home(kept[0], passed[0]), preferred_element_type=jnp.float32
    ) + jnp.einsum(
        "zxckr,zxcpqkd->rpxqd",
        homes[:, ::-1],
        send_home(kept[1], passed[1]),
        preferred_element_type=jnp.float32,
    )
    return (query_grad, encoded_grad.astype(jnp.bfloat16).reshape(stored_rows, -1))


def solution(mesh):
    in_specs = (
        P("dp", "tensor"),
        P("dp", "tensor"),
        P("dp"),
        P("dp", "tensor"),
        P("dp", None),
        P(None, "dp", "tensor"),
        P(None, "dp", "tensor"),
    )
    out_specs = (P("dp", "tensor"), P("dp", "tensor"))
    return jax.shard_map(
        on_device, mesh=mesh, in_specs=in_specs, out_specs=out_specs, check_vma=False
    )
```
